32 devices in a mesh: grp: 2 (over y), op: 4 (over z), sec: 2 (over x), rep: 2 (over core).
Axes of the slice: x: 2, y: 2, z: 4, core: 2. Of those that a mesh axis runs over, the one named last changes fastest.
Arguments:
- wavefunction: float32 [24, 256, 256], P(('grp', 'sec')), parts along dimension 0, may hold values from -6 to 6
- left_operators: float32 [64, 256, 256], P(('op', 'rep')), as said below
- right_operators: float32 [64, 256, 256], P(('op', 'rep')), as said below
- coupling: int32 [64, 12], P(('op', 'rep')), may hold values from 0 to 11, as said below
- left_sizes: int32 [24], P('grp'), parts along dimension 0, may hold values from 64 to 256, as said below
- right_sizes: int32 [24], P('grp'), parts along dimension 0, may hold values from 64 to 256, as said below
Outputs:
- sigma_next: float32 [24, 256, 256], P(('grp', 'sec'), ('op', 'rep')), parts along dimension 0
- residual: float32 [24, 256, 256], P(('grp', 'sec'), ('op', 'rep')), parts along dimension 0
The draws below stay inside these ranges and needn't reach their ends.
There are 2 independent parts, one for each index of `grp`. The reference program is written for one: setup_inputs(seed, part) draws one part's arguments, and reference() takes and returns one part's arrays. A program takes and returns all parts, laid end to end along the dimension named above; an argument that names none is the same for every part. Nothing has to cross between parts.
Inputs may be any that keep to these rules, and one draw needn't show every extreme that they name: `left_sizes`: in every draw one sector has exactly 256 rows and another exactly 64. `right_sizes`: in every draw one sector has exactly 256 columns and another exactly 64. `coupling`: every row is a permutation of the 12 sectors; row k + 32 is the inverse of row k for k below 32; a quarter of the rows or more are the identity. `left_operators`: term k + 32 is the transpose of term k for k below 32. `right_operators`: term k + 32 is the transpose of term k for k below 32.
All inputs are finite; a program needn't handle non-finite values.
Results may differ from the reference program's by a relative error of at most 0.00017.
Values sent between devices are 32-bit elements; how exact they have to be, the bound alone decides.
No kernel may reach another device: no remote copies, remote signals or barrier semaphores. Data moves between devices by JAX's collectives and lax.ppermute only.
A program may use at most 128 MiB of HBM per device.

```python
import jax
import jax.numpy as jnp
from jax import lax

B = 256
NSEC = 12
K = 64


def sector_places(key):
    where_full = jax.random.randint(jax.random.fold_in(key, 11), (), 0, NSEC)
    step_away = jax.random.randint(jax.random.fold_in(key, 17), (), 1, NSEC)
    where_small = (where_full + step_away) % NSEC
    return (where_full, where_small)


def sector_levels(key, top_place, low_place):
    levels = jax.random.randint(key, (NSEC,), B // 4, B + 1)
    levels = levels.at[top_place].set(B)
    levels = levels.at[low_place].set(B // 4)
    return levels.astype(jnp.int32)


def draw_left_sizes(key, part):
    first_place, second_place = sector_places(key)
    key = jax.random.fold_in(key, 3)
    return sector_levels(key, first_place, second_place)


def draw_right_sizes(key, part):
    first_place, second_place = sector_places(key)
    key = jax.random.fold_in(key, 5)
    return sector_levels(key, second_place, first_place)


def paired_terms(noise, gains, noise_scale, diag_scale):
    identity = jnp.eye(B, dtype=jnp.float32)
    half = noise * noise_scale + diag_scale * gains * identity[None, :, :]
    return jnp.concatenate([half, jnp.swapaxes(half, 1, 2)], axis=0).astype(jnp.float32)


def draw_left_operators(key, part):
    key = jax.random.fold_in(key, 7)
    noise_key, gain_key = jax.random.split(key)
    half_count = K // 2
    noise = jnp.clip(jax.random.normal(noise_key, (half_count, B, B), jnp.float32), -6.0, 6.0)
    gains = jnp.exp(jax.random.uniform(gain_key, (half_count, 1, 1), jnp.float32, -0.69, 0.69))
    return paired_terms(noise, gains, 1.0 / (B * K) ** 0.5, 0.5 / K ** 0.5)


def draw_right_operators(key, part):
    key = jax.random.fold_in(key, 9)
    noise_key, gain_key = jax.random.split(key)
    half_count = K // 2
    noise = jnp.clip(jax.random.normal(noise_key, (half_count, B, B), jnp.float32), -6.0, 6.0)
    gains = jnp.exp(jax.random.uniform(gain_key, (half_count, 1, 1), jnp.float32, -0.69, 0.69))
    return paired_terms(noise, gains, 1.0 / B ** 0.5, 1.0)


def one_permutation(row_key):
    return jax.random.permutation(row_key, NSEC)


def draw_coupling(key, part):
    key = jax.random.fold_in(key, 13)
    half_count = K // 2
    row_keys = jax.random.split(key, half_count)
    shuffled = jax.vmap(one_permutation)(row_keys).astype(jnp.int32)
    offset = jax.random.randint(jax.random.fold_in(key, 1), (), 0, 4)
    rows = jnp.arange(half_count, dtype=jnp.int32)
    drawn = jnp.broadcast_to(jnp.arange(NSEC, dtype=jnp.int32)[None, :], (half_count, NSEC))
    is_drawn = ((rows + offset) % 4 == 0)[:, None]
    first = jnp.where(is_drawn, drawn, shuffled).astype(jnp.int32)
    inverse = jnp.zeros((half_count, NSEC), jnp.int32).at[rows[:, None], first].set(drawn)
    return jnp.concatenate([first, inverse], axis=0).astype(jnp.int32)


def steps_of(rng, dims, pieces, least, high):
    def one(axis_at, blocks):
        heights = jax.random.uniform(jax.random.fold_in(jax.random.fold_in(rng, 6), axis_at), (blocks,), jnp.float32, least / len(pieces), high / len(pieces))
        return jnp.repeat(jnp.exp(heights), dims[axis_at] // blocks).reshape((-1,) + (1,) * (len(dims) - axis_at - 1))

    gain = one(*pieces[0])
    for cut in pieces[1:]:
        gain = gain * one(*cut)
    return gain


def normal_values(key, extent, deviation, reach, cuts=(), kind=jnp.bfloat16):
    loudness = steps_of(key, extent, cuts, -0.22, 0.18) if cuts else 1.0
    result = jax.random.normal(key, extent, jnp.float32) * deviation * loudness
    return jnp.minimum(jnp.maximum(result, -reach), reach).astype(kind)


def setup_inputs(seed: int = 0, part: int = 0) -> dict:
    key_list = jax.random.split(jax.random.key(seed), 7)
    part_keys = jax.random.split(jax.random.fold_in(key_list[6], part), 7)
    wavefunction = normal_values(part_keys[0], (NSEC, B, B), 1.0, 6.0, ((0, 2),), jnp.float32)
    left_operators = draw_left_operators(jax.random.fold_in(key_list[6], 71), part)
    right_operators = draw_right_operators(jax.random.fold_in(key_list[6], 71), part)
    coupling = draw_coupling(jax.random.fold_in(key_list[6], 71), part)
    left_sizes = draw_left_sizes(jax.random.fold_in(jax.random.fold_in(key_list[6], part), 71), part)
    right_sizes = draw_right_sizes(jax.random.fold_in(jax.random.fold_in(key_list[6], part), 71), part)
    return dict(wavefunction=wavefunction, left_operators=left_operators, right_operators=right_operators, coupling=coupling, left_sizes=left_sizes, right_sizes=right_sizes)


def build_mask(left_sizes, right_sizes):
    row_ids = jnp.arange(B, dtype=jnp.int32)
    row_ok = row_ids[None, :, None] < left_sizes[:, None, None]
    col_ok = row_ids[None, None, :] < right_sizes[:, None, None]
    return jnp.where(row_ok & col_ok, 1.0, 0.0).astype(jnp.float32)

def apply_hamiltonian(field, left_operators, right_operators, coupling, block_mask):

    def term_step(summed, term_items):
        left_op, right_op, source_ids = term_items
        picked = field[source_ids]
        halfway = jnp.einsum('ij,sjl->sil', left_op, picked, precision=lax.Precision.HIGHEST)
        product = jnp.einsum('sil,ml->sim', halfway, right_op, precision=lax.Precision.HIGHEST)
        return (summed + product, None)
    summed, _ = lax.scan(term_step, jnp.zeros(field.shape, jnp.float32), (left_operators, right_operators, coupling))
    return summed * block_mask

def reference(wavefunction, left_operators, right_operators, coupling, left_sizes, right_sizes):
    block_mask = build_mask(left_sizes, right_sizes)
    masked_wave = wavefunction * block_mask
    sigma_first = apply_hamiltonian(masked_wave, left_operators, right_operators, coupling, block_mask)
    energy = jnp.sum(masked_wave * sigma_first) / jnp.sum(masked_wave * masked_wave)
    residual = sigma_first - energy * masked_wave
    entries = residual.shape[0] * residual.shape[1] * residual.shape[2]
    direction = residual / jnp.sqrt(jnp.sum(residual * residual) / entries + 1e-06)
    sigma_next = apply_hamiltonian(direction, left_operators, right_operators, coupling, block_mask)
    return (sigma_next, residual)
```

```python
import functools

import jax
import jax.numpy as jnp
from jax import lax
from jax.experimental import pallas as pl
from jax.experimental.pallas import tpu as pltpu
from jax.sharding import PartitionSpec as P

F32 = jnp.float32
BF16 = jnp.bfloat16
CONTRACT_LAST = (((1,), (1,)), ((), ()))
CONTRACT_FIRST = (((1,), (0,)), ((), ()))
EVERYONE = ("grp", "op", "sec", "rep")


def halves(value):
    high = value.astype(BF16)
    low = (value - high.astype(F32)).astype(BF16)
    return high, low


def wide_left(pair, width):
    high, low = pair[:, :width], pair[:, width:]
    return jnp.concatenate([high, high, low], axis=1)


def wide_right(pair, width, axis):
    high, low = pair[:, :width], pair[:, width:]
    return jnp.concatenate([high, low, high], axis=axis)


class Plan:
    def __init__(self, mesh_shape, wavefunction, operators, coupling):
        self.grp, self.op, self.sec, self.rep = (mesh_shape[a] for a in EVERYONE)
        self.half = self.op // 2
        self.own, self.width = wavefunction.shape[0], wavefunction.shape[1]
        self.terms = operators.shape[0]
        self.sectors = coupling.shape[1]
        self.rows = self.width // (self.op * self.rep)
        self.part = self.width // 2

    def perm(self, move):
        def flat(g, o, s, r):
            return ((g * self.op + o) * self.sec + s) * self.rep + r

        pairs = []
        for g in range(self.grp):
            for o in range(self.op):
                for s in range(self.sec):
                    for r in range(self.rep):
                        to = move(o, s, r)
                        if to is not None:
                            pairs.append((flat(g, o, s, r), flat(g, *to)))
        return pairs

    def across_cores(self, x):
        return lax.ppermute(x, EVERYONE, self.perm(lambda o, s, r: (o, s, 1 - r)))

    def next_sec(self, x):
        return lax.ppermute(x, EVERYONE, self.perm(lambda o, s, r: (o, (s + 1) % self.sec, r)))

    def next_in_half(self, x):
        def move(o, s, r):
            base = o // self.half * self.half
            return (base + (o - base + 1) % self.half, s, r)

        return lax.ppermute(x, EVERYONE, self.perm(move))

    def flip_op(self, x, bits):
        return lax.ppermute(x, EVERYONE, self.perm(lambda o, s, r: (o ^ bits, s, r)))

    def flip_sec(self, x, bits):
        return lax.ppermute(x, EVERYONE, self.perm(lambda o, s, r: (o, s ^ bits, r)))

    def onward(self, x):
        to = {0: 2, 2: 3, 3: 1, 1: 0}
        return lax.ppermute(x, EVERYONE, self.perm(lambda o, s, r: (to[o], s, r)))


def places(plan):
    op = lax.axis_index("op")
    return lax.div(op, plan.half), lax.rem(op, plan.half), lax.axis_index("sec"), lax.axis_index("rep")


def invert_rows(plan, coupling, inverse):
    for k in range(plan.terms):
        for s in range(plan.sectors):
            inverse[k, coupling[k, s]] = s


def prepare_left(plan, half_at, operators, a_pair):
    w, h = plan.width, plan.part
    for k in range(plan.terms):
        high, low = halves(operators[k, pl.ds(half_at, h), :])
        a_pair[k, :, :w], a_pair[k, :, w:] = high, low
        high, low = halves(operators[k, :, pl.ds(half_at, h)].T)
        a_pair[plan.terms + k, :, :w], a_pair[plan.terms + k, :, w:] = high, low


def prepare_right(plan, operators, b_pair):
    w = plan.width
    for k in range(plan.terms):
        high, low = halves(operators[k])
        b_pair[k, :, :w], b_pair[k, :, w:] = high, low


def apply_terms(plan, my_sec, coupling, inverse, a_pair, b_pair, s_pair, u_pair, total):
    w, h, terms, own = plan.width, plan.part, plan.terms, plan.own
    total[...] = jnp.zeros_like(total)

    def first_stage(t, carry):
        weights = wide_right(s_pair[t], w, 1)
        for side in range(2):
            left = a_pair[side * terms:(side + 1) * terms].reshape(terms * h, 2 * w)
            got = lax.dot_general(wide_left(left, w), weights, CONTRACT_LAST, preferred_element_type=F32)
            high, low = halves(got)
            for k in range(terms):
                at = pl.ds(pl.multiple_of(t * h, h), h)
                u_pair[side * terms + k, at, :w] = high[k * h:(k + 1) * h]
                u_pair[side * terms + k, at, w:] = low[k * h:(k + 1) * h]
        return carry

    lax.fori_loop(0, own, first_stage, 0)

    def second_stage(k, carry):
        first_own = my_sec * own
        left = wide_left(u_pair[k], w)
        got = lax.dot_general(left, wide_right(b_pair[k], w, 1), CONTRACT_LAST, preferred_element_type=F32)
        for t in range(own):
            total[inverse[k, first_own + t]] += got[t * h:(t + 1) * h]
        left = wide_left(u_pair[terms + k], w)
        got = lax.dot_general(left, wide_right(b_pair[k], w, 0), CONTRACT_FIRST, preferred_element_type=F32)
        for t in range(own):
            total[coupling[k, first_own + t]] += got[t * h:(t + 1) * h]
        return carry

    lax.fori_loop(0, terms, second_stage, 0)


def hand_out(plan, total, row_sizes, col_sizes, keep, send):
    side, mine, my_sec, my_rep = places(plan)
    row_id = lax.broadcasted_iota(jnp.int32, (plan.rows, plan.width), 0)
    col_id = lax.broadcasted_iota(jnp.int32, (plan.rows, plan.width), 1)
    for sec_off in range(plan.sec):
        for op_off in range(plan.half):
            for rep_off in range(plan.rep):
                at = (lax.rem(mine + op_off, plan.half) * plan.rep + lax.rem(my_rep + rep_off, plan.rep)) * plan.rows
                at = pl.multiple_of(at, plan.rows)
                goal = send if rep_off else keep
                for t in range(plan.own):
                    s = lax.rem(my_sec + sec_off, plan.sec) * plan.own + t
                    ok = (row_id + (side * plan.part + at) < row_sizes[s]) & (col_id < col_sizes[s])
                    goal[sec_off, op_off, t] = jnp.where(ok, total[s, pl.ds(at, plan.rows), :], 0.0)


def start_loads(pairs, sems):
    copies = [pltpu.make_async_copy(src, dst, sems.at[i]) for i, (src, dst) in enumerate(pairs)]
    for copy in copies:
        copy.start()
    return copies


def first_kernel(plan, coupling, left_sizes, right_sizes, wave, left_ops, right_ops,
                 keep, send, turned, piece,
                 wave_in, left_in, right_in, a_pair, b_pair, s_pair, u_pair, total, inverse, sems):
    side, mine, my_sec, my_rep = places(plan)
    copies = start_loads([(wave, wave_in), (right_ops, right_in), (left_ops, left_in)], sems)
    invert_rows(plan, coupling, inverse)
    w = plan.width
    copies[0].wait()
    row_id = lax.broadcasted_iota(jnp.int32, (w, w), 0)
    col_id = lax.broadcasted_iota(jnp.int32, (w, w), 1)
    at = pl.multiple_of((lax.axis_index("op") * plan.rep + my_rep) * plan.rows, plan.rows)
    for t in range(plan.own):
        s = my_sec * plan.own + t
        ok = (row_id < left_sizes[s]) & (col_id < right_sizes[s])
        masked = jnp.where(ok, wave_in[t], 0.0)
        high, low = halves(masked)
        s_pair[t, :, :w], s_pair[t, :, w:] = high, low
        turned[t] = masked.T
        piece[t] = turned[t, pl.ds(at, plan.rows), :]
    copies[1].wait()
    prepare_left(plan, pl.multiple_of(side * plan.part, plan.part), right_in, a_pair)
    copies[2].wait()
    prepare_right(plan, left_in, b_pair)
    apply_terms(plan, my_sec, coupling, inverse, a_pair, b_pair, s_pair, u_pair, total)
    hand_out(plan, total, right_sizes, left_sizes, keep, send)


def second_kernel(plan, coupling, left_sizes, right_sizes, scalars, turned, left_ops, right_ops, *rest):
    units, rest = rest[:2 * plan.op], rest[2 * plan.op:]
    (keep, send, residual, norm,
     turned_in, left_in, right_in, source, a_pair, b_pair, s_pair, u_pair, total, inverse, sems) = rest
    side, mine, my_sec, my_rep = places(plan)
    my_op = lax.axis_index("op")
    copies = start_loads([(turned, turned_in), (left_ops, left_in), (right_ops, right_in)], sems)
    invert_rows(plan, coupling, inverse)
    w, rows = plan.width, plan.rows

    for whose in range(2):
        for bits in range(plan.op):
            unit = units[whose * plan.op + bits]
            r = my_rep if whose == 0 else 1 - my_rep
            at = pl.multiple_of(((my_op ^ bits) * plan.rep + r) * rows, rows)
            for t in range(plan.own):
                source[t, pl.ds(at, rows), :] = unit[t]

    energy, level = scalars[0], scalars[1]
    copies[0].wait()
    at = pl.multiple_of((mine * plan.rep + my_rep) * rows, rows)
    half_at = pl.multiple_of(side * plan.part, plan.part)
    squares = jnp.zeros((8, w), F32)
    for t in range(plan.own):
        res = source[t] - energy * turned_in[t]
        squares = squares + jnp.sum((res * res).reshape(w // 8, 8, w), axis=0)
        source[t] = res
        u_rows = source[t, :, pl.ds(half_at, plan.part)].T
        total[t] = u_rows
        residual[t] = total[t, pl.ds(at, rows), :]
        high, low = halves(res * level)
        s_pair[t, :, :w], s_pair[t, :, w:] = high, low
    norm[...] = jnp.full(norm.shape, jnp.sum(squares), F32)
    copies[1].wait()
    prepare_left(plan, half_at, left_in, a_pair)
    copies[2].wait()
    prepare_right(plan, right_in, b_pair)
    apply_terms(plan, my_sec, coupling, inverse, a_pair, b_pair, s_pair, u_pair, total)
    hand_out(plan, total, left_sizes, right_sizes, keep, send)


def common_scratch(plan):
    w, h = plan.width, plan.part
    return [
        pltpu.VMEM((2 * plan.terms, h, 2 * w), BF16),
        pltpu.VMEM((plan.terms, w, 2 * w), BF16),
        pltpu.VMEM((plan.own, w, 2 * w), BF16),
        pltpu.VMEM((2 * plan.terms, plan.own * h, 2 * w), BF16),
        pltpu.VMEM((plan.sectors, h, w), F32),
        pltpu.SMEM((plan.terms, plan.sectors), jnp.int32),
        pltpu.SemaphoreType.DMA((3,)),
    ]


def sum_over_owners(plan, keep, send):
    both = keep + plan.across_cores(send)
    sums = [None] * plan.sec
    for sec_off in list(range(1, plan.sec)) + [0]:
        run = both[sec_off, plan.half - 1]
        for op_off in range(plan.half - 2, -1, -1):
            run = plan.next_in_half(run) + both[sec_off, op_off]
        sums[sec_off] = run
    run = sums[plan.sec - 1]
    for sec_off in range(plan.sec - 2, -1, -1):
        run = plan.next_sec(run) + sums[sec_off]
    return run


def powers(count):
    return [1 << i for i in range(count.bit_length() - 1)]


def total_of(plan, x):
    x = x + plan.across_cores(x)
    for bits in powers(plan.sec):
        x = x + plan.flip_sec(x, bits)
    for bits in powers(plan.op):
        x = x + plan.flip_op(x, bits)
    return x


def gather_along_op(plan, piece):
    if plan.op == 4:
        far = plan.flip_op(piece, 3)
        near = plan.flip_op(piece, 1)
        op = lax.axis_index("op")
        carried = jnp.where((op == 1) | (op == 2), far, piece)
        return [piece, near, plan.onward(carried), far]
    got = piece[None]
    for bits in powers(plan.op):
        got = jnp.concatenate([got, plan.flip_op(got, bits)])
    return [got[i] for i in range(plan.op)]


def on_device(mesh_shape, wavefunction, left_operators, right_operators, coupling, left_sizes, right_sizes):
    plan = Plan(mesh_shape, wavefunction, left_operators, coupling)
    own, w, rows = plan.own, plan.width, plan.rows
    smem = pl.BlockSpec(memory_space=pltpu.SMEM)
    vmem = pl.BlockSpec(memory_space=pltpu.VMEM)
    anywhere = pl.BlockSpec(memory_space=pl.ANY)
    spread = jax.ShapeDtypeStruct((plan.sec, plan.half, own, rows, w), F32)
    whole = jax.ShapeDtypeStruct((own, w, w), F32)
    chunk = jax.ShapeDtypeStruct((own, rows, w), F32)
    operators = pltpu.VMEM((plan.terms, w, w), F32)
    blocks = pltpu.VMEM((own, w, w), F32)
    flops = 3 * 2 * 2 * 2 * plan.terms * own * plan.part * w * w
    cost = pl.CostEstimate(flops=flops, bytes_accessed=8 << 20, transcendentals=0)
    params = pltpu.CompilerParams(vmem_limit_bytes=40 << 20)

    keep, send, turned, piece = pl.pallas_call(
        functools.partial(first_kernel, plan),
        out_shape=(spread, spread, whole, chunk),
        in_specs=[smem] * 3 + [anywhere] * 3,
        out_specs=(vmem,) * 4,
        scratch_shapes=[blocks, operators, operators] + common_scratch(plan),
        compiler_params=params,
        cost_estimate=cost,
    )(coupling, left_sizes, right_sizes, wavefunction, left_operators, right_operators)

    sigma = sum_over_owners(plan, keep, send)

    units = gather_along_op(plan, sigma)
    units = units + [plan.across_cores(unit) for unit in units]

    entries = plan.sectors * w * w
    tiny = 2.0 ** -32
    sums = [jnp.sum(piece * sigma), jnp.sum(piece * piece), jnp.sum((sigma * tiny) ** 2)]
    sums = total_of(plan, jnp.stack([jnp.full((8, 128), x) for x in sums]))[:, 0, 0]
    energy = sums[0] / sums[1]
    height = 1.0 + jnp.sqrt(sums[2] / entries) / tiny
    scalars = jnp.stack([energy, 1.0 / height])

    keep, send, residual, norm = pl.pallas_call(
        functools.partial(second_kernel, plan),
        out_shape=(spread, spread, chunk, jax.ShapeDtypeStruct((8, 128), F32)),
        in_specs=[smem] * 4 + [anywhere] * 3 + [vmem] * len(units),
        out_specs=(vmem,) * 4,
        scratch_shapes=[blocks, operators, operators, blocks] + common_scratch(plan),
        compiler_params=params,
        cost_estimate=cost,
    )(coupling, left_sizes, right_sizes, scalars, turned, left_operators, right_operators, *units)

    moving = norm
    for _ in range(1, plan.sec):
        moving = plan.next_sec(moving)
        norm = norm + moving
    factor = height / jnp.sqrt(norm[0, 0] / entries + 1e-06)
    sigma_next = sum_over_owners(plan, keep, send) * factor
    return (sigma_next, residual)


def solution(mesh):
    in_specs = (
        P(("grp", "sec"), None, None),
        P(("op", "rep"), None, None),
        P(("op", "rep"), None, None),
        P(("op", "rep"), None),
        P("grp"),
        P("grp"),
    )
    out_specs = (P(("grp", "sec"), ("op", "rep"), None), P(("grp", "sec"), ("op", "rep"), None))
    return jax.shard_map(
        functools.partial(on_device, dict(mesh.shape)),
        mesh=mesh, in_specs=in_specs, out_specs=out_specs, check_vma=False,
    )
```

```python
import functools

import jax
import jax.numpy as jnp
from jax import lax
from jax.experimental import pallas as pl
from jax.experimental.pallas import tpu as pltpu
from jax.sharding import PartitionSpec as P

F32 = jnp.float32
BF16 = jnp.bfloat16
CONTRACT_LAST = (((1,), (1,)), ((), ()))
CONTRACT_FIRST = (((1,), (0,)), ((), ()))
EVERYONE = ("grp", "op", "sec", "rep")
TINY = 2.0 ** -32
TILE = 8


def halves(value):
    high = value.astype(BF16)
    low = (value - high.astype(F32)).astype(BF16)
    return high, low


def put_halves(goal, at, value):
    width = value.shape[-1]
    goal[at + (slice(0, width),)], goal[at + (slice(width, 2 * width),)] = halves(value)


def wide_left(pair, width):
    high, low = pair[:, :width], pair[:, width:]
    return jnp.concatenate([high, high, low], axis=1)


def wide_right(pair, width, axis):
    high, low = pair[:, :width], pair[:, width:]
    return jnp.concatenate([high, low, high], axis=axis)


def powers(count):
    return [1 << i for i in range(count.bit_length() - 1)]


class Plan:
    def __init__(self, mesh_shape, wavefunction, operators, coupling):
        self.grp, self.op, self.sec, self.rep = (mesh_shape[a] for a in EVERYONE)
        self.half = self.op // 2
        self.own, self.width = wavefunction.shape[0], wavefunction.shape[1]
        self.terms = operators.shape[0]
        self.sectors = coupling.shape[1]
        self.rows = self.width // (self.op * self.rep)
        self.block = self.rows * self.rep
        self.part = self.width // 2
        self.away = self.block * (self.half - 1)
        self.piece = self.own * self.rows

    def perm(self, move):
        def flat(g, o, s, r):
            return ((g * self.op + o) * self.sec + s) * self.rep + r

        pairs = []
        for g in range(self.grp):
            for o in range(self.op):
                for s in range(self.sec):
                    for r in range(self.rep):
                        pairs.append((flat(g, o, s, r), flat(g, *move(o, s, r))))
        return pairs

    def across_cores(self, x):
        return lax.ppermute(x, EVERYONE, self.perm(lambda o, s, r: (o, s, 1 - r)))

    def next_sec(self, x):
        return lax.ppermute(x, EVERYONE, self.perm(lambda o, s, r: (o, (s + 1) % self.sec, r)))

    def next_in_half(self, x):
        def move(o, s, r):
            base = o // self.half * self.half
            return (base + (o - base + 1) % self.half, s, r)

        return lax.ppermute(x, EVERYONE, self.perm(move))

    def flip_op(self, x, bits):
        return lax.ppermute(x, EVERYONE, self.perm(lambda o, s, r: (o ^ bits, s, r)))

    def flip_sec(self, x, bits):
        return lax.ppermute(x, EVERYONE, self.perm(lambda o, s, r: (o, s ^ bits, r)))

    def onward(self, x):
        to = {0: 2, 2: 3, 3: 1, 1: 0}
        return lax.ppermute(x, EVERYONE, self.perm(lambda o, s, r: (to[o], s, r)))


def places(plan):
    op = lax.axis_index("op")
    return lax.div(op, plan.half), lax.rem(op, plan.half), lax.axis_index("sec"), lax.axis_index("rep")


def prepare(plan, left_in, right_in, flipped, a_away, a_home, b_pair, ready):
    side, mine, _, _ = places(plan)
    half_at = pl.multiple_of(side * plan.part, plan.part)
    ready(0)
    for k in range(plan.terms):
        flipped[k] = left_in[k, :, pl.ds(half_at, plan.part)].T
    for off in range(plan.half):
        at = pl.multiple_of(lax.rem(mine + off, plan.half) * plan.block, plan.block)
        goal = a_away if off else a_home
        start = (off - 1) * plan.block if off else 0
        rows = slice(start, start + plan.block)
        for k in range(plan.terms):
            straight = left_in[k, pl.ds(pl.multiple_of(half_at + at, plan.block), plan.block), :]
            put_halves(goal, (k, rows), straight)
            put_halves(goal, (plan.terms + k, rows), flipped[k, pl.ds(at, plan.block), :])
    ready(1)
    for k in range(plan.terms):
        put_halves(b_pair, (k, slice(None)), right_in[k])


def apply_terms(plan, coupling, inverse, a_pair, b_pair, s_pair, u_pair, total):
    w, terms, own = plan.width, plan.terms, plan.own
    n = a_pair.shape[1]
    first_own = lax.axis_index("sec") * own
    for k in range(terms):
        for s in range(plan.sectors):
            inverse[k, coupling[k, s]] = s
    total[...] = jnp.zeros_like(total)
    left = wide_left(a_pair[...].reshape(2 * terms * n, 2 * w), w)
    for t in range(own):
        got = lax.dot_general(left, wide_right(s_pair[t], w, 1), CONTRACT_LAST, preferred_element_type=F32)
        high, low = halves(got)
        for k in range(2 * terms):
            u_pair[k, t * n:(t + 1) * n, :w] = high[k * n:(k + 1) * n]
            u_pair[k, t * n:(t + 1) * n, w:] = low[k * n:(k + 1) * n]

    unroll = 8 if terms % 8 == 0 else 1

    def second_stage(i, carry):
        for j in range(unroll):
            k = i * unroll + j
            got = lax.dot_general(wide_left(u_pair[k], w), wide_right(b_pair[k], w, 1), CONTRACT_LAST,
                                  preferred_element_type=F32)
            for t in range(own):
                total[inverse[k, first_own + t]] += got[t * n:(t + 1) * n]
            got = lax.dot_general(wide_left(u_pair[terms + k], w), wide_right(b_pair[k], w, 0), CONTRACT_FIRST,
                                  preferred_element_type=F32)
            for t in range(own):
                total[coupling[k, first_own + t]] += got[t * n:(t + 1) * n]
        return carry

    lax.fori_loop(0, terms // unroll, second_stage, 0)


def hand_out(plan, offsets, total, row_sizes, col_sizes, keep, send):
    side, mine, my_sec, my_rep = places(plan)
    rows = plan.rows
    row_id = lax.broadcasted_iota(jnp.int32, (rows, plan.width), 0)
    col_id = lax.broadcasted_iota(jnp.int32, (rows, plan.width), 1)
    for sec_off in range(plan.sec):
        for i, op_off in enumerate(offsets):
            for rep_off in range(plan.rep):
                inner = pl.multiple_of(lax.rem(my_rep + rep_off, plan.rep) * rows, rows)
                first_row = side * plan.part + lax.rem(mine + op_off, plan.half) * plan.block + inner
                goal = send if rep_off else keep
                for t in range(plan.own):
                    s = lax.rem(my_sec + sec_off, plan.sec) * plan.own + t
                    ok = (row_id + first_row < row_sizes[s]) & (col_id < col_sizes[s])
                    value = total[s, pl.ds(pl.multiple_of(i * plan.block + inner, rows), rows), :]
                    goal[sec_off, i, t * rows:(t + 1) * rows] = jnp.where(ok, value, 0.0)


def first_kernel(plan, coupling, left_sizes, right_sizes, wave, left_ops, right_ops,
                 keep, send, turned, piece, a_home, b_pair, s_pair,
                 wave_in, left_in, right_in, flipped, a_away, u_pair, total, inverse, sems):
    _, _, my_sec, my_rep = places(plan)
    w = plan.width
    loads = ((wave, wave_in), (right_ops, right_in), (left_ops, left_in))
    copies = [pltpu.make_async_copy(src, dst, sems.at[i]) for i, (src, dst) in enumerate(loads)]
    for copy in copies:
        copy.start()
    copies[0].wait()
    row_id = lax.broadcasted_iota(jnp.int32, (w, w), 0)
    col_id = lax.broadcasted_iota(jnp.int32, (w, w), 1)
    at = pl.multiple_of((lax.axis_index("op") * plan.rep + my_rep) * plan.rows, plan.rows)
    for t in range(plan.own):
        s = my_sec * plan.own + t
        ok = (row_id < left_sizes[s]) & (col_id < right_sizes[s])
        masked = jnp.where(ok, wave_in[t], 0.0)
        put_halves(s_pair, (t, slice(None)), masked)
        turned[t] = masked.T
        piece[t * plan.rows:(t + 1) * plan.rows] = turned[t, pl.ds(at, plan.rows), :]
    prepare(plan, right_in, left_in, flipped, a_away, a_home, b_pair, lambda i: copies[1 + i].wait())
    apply_terms(plan, coupling, inverse, a_away, b_pair, s_pair, u_pair, total)
    hand_out(plan, range(1, plan.half), total, right_sizes, left_sizes, keep, send)


def home_kernel(plan, coupling, row_sizes, col_sizes, a_home, b_pair, s_pair, keep, send, u_pair, total, inverse):
    apply_terms(plan, coupling, inverse, a_home, b_pair, s_pair, u_pair, total)
    hand_out(plan, range(1), total, row_sizes, col_sizes, keep, send)


def prepare_kernel(plan, left_ops, right_ops, a_away, a_home, b_pair, flipped):
    prepare(plan, left_ops, right_ops, flipped, a_away, a_home, b_pair, lambda i: None)


def second_kernel(plan, coupling, left_sizes, right_sizes, turned, a_away, b_pair, *rest):
    units, rest = rest[:2 * plan.op], rest[2 * plan.op:]
    (keep, send, s_pair, residual, norm, source, flipped, u_pair, total, inverse) = rest
    side, mine, _, my_rep = places(plan)
    my_op = lax.axis_index("op")
    w, rows = plan.width, plan.rows
    sums = jnp.zeros((TILE, w), F32)
    for whose in range(2):
        for bits in range(plan.op):
            unit = units[whose * plan.op + bits]
            r = my_rep if whose == 0 else 1 - my_rep
            at = pl.multiple_of(((my_op ^ bits) * plan.rep + r) * rows, rows)
            for t in range(plan.own):
                source[t, pl.ds(at, rows), :] = unit[t * rows:(t + 1) * rows]
            sums = sums + unit[plan.piece:]
    entries = plan.sectors * w * w
    sums = jnp.broadcast_to(jnp.sum(sums, axis=1, keepdims=True), sums.shape)
    energy = sums[0:1] / sums[1:2]
    height = 1.0 + jnp.sqrt(sums[2:3] / entries) / TINY
    level = 1.0 / height
    at = pl.multiple_of((mine * plan.rep + my_rep) * rows, rows)
    half_at = pl.multiple_of(side * plan.part, plan.part)
    squares = jnp.zeros((8, w), F32)
    for t in range(plan.own):
        res = source[t] - energy * turned[t]
        squares = squares + jnp.sum((res * res).reshape(w // 8, 8, w), axis=0)
        source[t] = res
        put_halves(s_pair, (t, slice(None)), res * level)
    for t in range(plan.own):
        flipped[t] = source[t, :, pl.ds(half_at, plan.part)].T
        residual[t] = flipped[t, pl.ds(at, rows), :]
    norm[0:4] = jnp.full((4, w), jnp.sum(squares), F32)
    norm[4:8] = jnp.broadcast_to(height, (4, w))
    apply_terms(plan, coupling, inverse, a_away, b_pair, s_pair, u_pair, total)
    hand_out(plan, range(1, plan.half), total, left_sizes, right_sizes, keep, send)


def sums_tile(products, squares, shares):
    rows = [sum(jnp.sum(x, axis=0, keepdims=True) for x in part) for part in (products, squares, shares)]
    return jnp.concatenate(rows + [jnp.zeros((TILE - 3,) + rows[0].shape[1:], F32)])


def gather_along_op(plan, piece, beside):
    if plan.op == 4:
        far = plan.flip_op(piece, 3)
        near = plan.flip_op(piece, 1)
        op = lax.axis_index("op")
        far, beside = lax.optimization_barrier((far, beside))
        carried = jnp.where((op == 1) | (op == 2), far, piece)
        return [piece, near, plan.onward(carried), far], beside
    got = piece[None]
    for bits in powers(plan.op):
        got = jnp.concatenate([got, plan.flip_op(got, bits)])
    return [got[i] for i in range(plan.op)], beside


def on_device(mesh_shape, wavefunction, left_operators, right_operators, coupling, left_sizes, right_sizes):
    plan = Plan(mesh_shape, wavefunction, left_operators, coupling)
    own, w, rows, terms = plan.own, plan.width, plan.rows, plan.terms
    smem = pl.BlockSpec(memory_space=pltpu.SMEM)
    vmem = pl.BlockSpec(memory_space=pltpu.VMEM)
    hbm = pl.BlockSpec(memory_space=pltpu.HBM)

    def spread(offsets):
        return jax.ShapeDtypeStruct((plan.sec, offsets, plan.piece, w), F32)

    def work(n):
        return [
            pltpu.VMEM((2 * terms, own * n, 2 * w), BF16),
            pltpu.VMEM((plan.sectors, n, w), F32),
            pltpu.SMEM((terms, plan.sectors), jnp.int32),
        ]

    def call(body, n, out_shape, in_specs, scratch, grant=36):
        flops = 3 * 2 * 2 * 2 * terms * own * n * w * w
        return pl.pallas_call(
            functools.partial(body, plan),
            out_shape=out_shape,
            in_specs=in_specs,
            out_specs=(vmem,) * len(out_shape),
            scratch_shapes=scratch,
            compiler_params=pltpu.CompilerParams(vmem_limit_bytes=grant << 20),
            cost_estimate=pl.CostEstimate(flops=flops, bytes_accessed=4 << 20, transcendentals=0),
        )

    blocks = jax.ShapeDtypeStruct((own, w, w), F32)
    block_pairs = jax.ShapeDtypeStruct((own, w, 2 * w), BF16)
    lefts_away = jax.ShapeDtypeStruct((2 * terms, plan.away, 2 * w), BF16)
    lefts_home = jax.ShapeDtypeStruct((2 * terms, plan.block, 2 * w), BF16)
    rights = jax.ShapeDtypeStruct((terms, w, 2 * w), BF16)
    chunk = jax.ShapeDtypeStruct((plan.piece, w), F32)
    operators = pltpu.VMEM((terms, w, w), F32)
    turned_operators = pltpu.VMEM((terms, plan.part, w), F32)
    home = call(home_kernel, plan.block, (spread(1),) * 2, [smem] * 3 + [vmem] * 3, work(plan.block))

    def along_half(keep, send, home_args, beside=()):
        away = keep + plan.across_cores(send)
        away, home_args = lax.optimization_barrier((away, home_args))
        run = away[:, plan.half - 2]
        for i in range(plan.half - 3, -1, -1):
            run = plan.next_in_half(run) + away[:, i]
        run = plan.next_in_half(run)
        home_keep, home_send = home(*home_args)
        home_send, beside = lax.optimization_barrier((home_send, beside))
        return run + (home_keep + plan.across_cores(home_send))[:, 0], beside

    def along_sec(sums, extra):
        run = sums[plan.sec - 1]
        if plan.sec == 2:
            return jnp.concatenate([sums[0], extra]) + plan.next_sec(jnp.concatenate([run, extra]))
        for i in range(plan.sec - 2, -1, -1):
            run = plan.next_sec(run) + sums[i]
        for bits in powers(plan.sec):
            extra = extra + plan.flip_sec(extra, bits)
        return jnp.concatenate([run, extra])

    keep, send, turned, piece, a_home, b_pair, s_pair = call(
        first_kernel, plan.away,
        (spread(plan.half - 1),) * 2 + (blocks, chunk, lefts_home, rights, block_pairs),
        [smem] * 3 + [hbm] * 3,
        [pltpu.VMEM(blocks.shape, F32), operators, operators, turned_operators,
         pltpu.VMEM(lefts_away.shape, BF16)] + work(plan.away) + [pltpu.SemaphoreType.DMA((3,))],
        grant=48,
    )(coupling, left_sizes, right_sizes, wavefunction, left_operators, right_operators)

    pieces = [piece]
    for _ in range(1, plan.sec):
        pieces.append(plan.next_sec(pieces[-1]))
    pieces = [pieces[-i % plan.sec] for i in range(plan.sec)]
    sums, pieces = along_half(keep, send, (coupling, right_sizes, left_sizes, a_home, b_pair, s_pair), pieces)
    extra = sums_tile(
        [pieces[i] * sums[i] for i in range(plan.sec)], [piece * piece],
        [(sums[i] * TINY) ** 2 for i in range(plan.sec)],
    )
    unit = along_sec(sums, extra)

    unit, left_again, right_again = lax.optimization_barrier((unit, left_operators, right_operators))
    prepared = call(
        prepare_kernel, 1, (lefts_away, lefts_home, rights), [vmem] * 2, [turned_operators],
    )(left_again, right_again)
    units, (a_away, a_home, b_pair) = gather_along_op(plan, unit, prepared)
    units = units + [plan.across_cores(x) for x in units]

    keep, send, s_pair, residual, norm = call(
        second_kernel, plan.away,
        (spread(plan.half - 1),) * 2 + (block_pairs, jax.ShapeDtypeStruct((own, rows, w), F32),
                                        jax.ShapeDtypeStruct((TILE, w), F32)),
        [smem] * 3 + [vmem] * (3 + len(units)),
        [pltpu.VMEM(blocks.shape, F32), pltpu.VMEM((own, plan.part, w), F32)] + work(plan.away),
    )(coupling, left_sizes, right_sizes, turned, a_away, b_pair, *units)

    sums, _ = along_half(keep, send, (coupling, left_sizes, right_sizes, a_home, b_pair, s_pair))
    done = along_sec(sums, norm)
    height = norm[4:5]
    entries = plan.sectors * w * w
    factor = height / jnp.sqrt(done[plan.piece:plan.piece + 1] / entries + 1e-06)
    sigma_next = (done[:plan.piece] * factor).reshape(own, rows, w)
    return (sigma_next, residual)


def solution(mesh):
    in_specs = (
        P(("grp", "sec"), None, None),
        P(("op", "rep"), None, None),
        P(("op", "rep"), None, None),
        P(("op", "rep"), None),
        P("grp"),
        P("grp"),
    )
    out_specs = (P(("grp", "sec"), ("op", "rep"), None), P(("grp", "sec"), ("op", "rep"), None))
    return jax.shard_map(
        functools.partial(on_device, dict(mesh.shape)),
        mesh=mesh, in_specs=in_specs, out_specs=out_specs, check_vma=False,
    )
```

```python
import functools

import jax
import jax.numpy as jnp
from jax import lax
from jax.experimental import pallas as pl
from jax.experimental.pallas import tpu as pltpu
from jax.sharding import PartitionSpec as P

F32 = jnp.float32
BF16 = jnp.bfloat16
CONTRACT_LAST = (((1,), (1,)), ((), ()))
CONTRACT_FIRST = (((1,), (0,)), ((), ()))
EVERYONE = ("grp", "op", "sec", "rep")
TINY = 2.0 ** -32
TILE = 8


def halves(value):
    high = value.astype(BF16)
    low = (value - high.astype(F32)).astype(BF16)
    return high, low


def wide_left(pair, width):
    high, low = pair[:, :width], pair[:, width:]
    return jnp.concatenate([high, high, low], axis=1)


def wide_right(pair, width, axis):
    high, low = pair[:, :width], pair[:, width:]
    return jnp.concatenate([high, low, high], axis=axis)


def powers(count):
    return [1 << i for i in range(count.bit_length() - 1)]


class Plan:
    def __init__(self, mesh_shape, wavefunction, operators, coupling):
        self.grp, self.op, self.sec, self.rep = (mesh_shape[a] for a in EVERYONE)
        self.half = self.op // 2
        self.own, self.width = wavefunction.shape[0], wavefunction.shape[1]
        self.terms = operators.shape[0]
        self.sectors = coupling.shape[1]
        self.rows = self.width // (self.op * self.rep)
        self.block = self.rows * self.rep
        self.part = self.width // 2
        self.away = self.block * (self.half - 1)
        self.piece = self.own * self.rows

    def perm(self, move):
        def flat(g, o, s, r):
            return ((g * self.op + o) * self.sec + s) * self.rep + r

        pairs = []
        for g in range(self.grp):
            for o in range(self.op):
                for s in range(self.sec):
                    for r in range(self.rep):
                        pairs.append((flat(g, o, s, r), flat(g, *move(o, s, r))))
        return pairs

    def across_cores(self, x):
        return lax.ppermute(x, EVERYONE, self.perm(lambda o, s, r: (o, s, 1 - r)))

    def next_sec(self, x):
        return lax.ppermute(x, EVERYONE, self.perm(lambda o, s, r: (o, (s + 1) % self.sec, r)))

    def next_in_half(self, x):
        def move(o, s, r):
            base = o // self.half * self.half
            return (base + (o - base + 1) % self.half, s, r)

        return lax.ppermute(x, EVERYONE, self.perm(move))

    def flip_op(self, x, bits):
        return lax.ppermute(x, EVERYONE, self.perm(lambda o, s, r: (o ^ bits, s, r)))

    def flip_sec(self, x, bits):
        return lax.ppermute(x, EVERYONE, self.perm(lambda o, s, r: (o, s ^ bits, r)))

    def onward(self, x):
        to = {0: 2, 2: 3, 3: 1, 1: 0}
        return lax.ppermute(x, EVERYONE, self.perm(lambda o, s, r: (to[o], s, r)))


def places(plan):
    op = lax.axis_index("op")
    return lax.div(op, plan.half), lax.rem(op, plan.half), lax.axis_index("sec"), lax.axis_index("rep")


class Stack:
    def __init__(self, ref, start, count, height):
        self.ref, self.start, self.count, self.height = ref, start, count, height

    def span(self, block, rows=None):
        first, last = (0, self.height) if rows is None else rows
        return slice(self.start + block * self.height + first, self.start + block * self.height + last)

    def put(self, block, value, rows=None):
        width = value.shape[-1]
        at = self.span(block, rows)
        self.ref[at, :width], self.ref[at, width:] = halves(value)

    def get(self, block):
        if isinstance(block, int):
            return self.ref[self.span(block)]
        return self.ref[pl.ds(pl.multiple_of(self.start + block * self.height, 16), self.height)]

    def all(self):
        return self.ref[self.start:self.start + self.count * self.height]


def stacks(plan, ref, *names):
    sizes = dict(
        away=(2 * plan.terms, plan.away), home=(2 * plan.terms, plan.block),
        right=(plan.terms, plan.width), source=(plan.own, plan.width),
    )
    found, start = [], 0
    for name in names:
        count, height = sizes[name]
        found.append(Stack(ref, start, count, height))
        start += count * height
    return found


def stack_shape(plan, *names):
    end = stacks(plan, None, *names)[-1]
    return (end.start + end.count * end.height, 2 * plan.width)


def prepare_left(plan, left_in, flipped, away, home):
    side, mine, _, _ = places(plan)
    half_at = pl.multiple_of(side * plan.part, plan.part)
    for k in range(plan.terms):
        flipped[k] = left_in[k, :, pl.ds(half_at, plan.part)].T
    for off in range(plan.half):
        at = pl.multiple_of(lax.rem(mine + off, plan.half) * plan.block, plan.block)
        goal = away if off else home
        start = (off - 1) * plan.block if off else 0
        rows = (start, start + plan.block)
        for k in range(plan.terms):
            goal.put(k, left_in[k, pl.ds(pl.multiple_of(half_at + at, plan.block), plan.block), :], rows)
            goal.put(plan.terms + k, flipped[k, pl.ds(at, plan.block), :], rows)


def prepare_right(plan, right_in, right):
    for k in range(plan.terms):
        right.put(k, right_in[k])


def apply_terms(plan, tables, inverse, lefts, right, source, u_pair, total):
    w, terms, own = plan.width, plan.terms, plan.own
    n = lefts.height
    first_own = lax.axis_index("sec") * own
    for k in range(terms):
        for s in range(plan.sectors):
            inverse[k, tables[k, s]] = s
    total[...] = jnp.zeros_like(total)
    left = wide_left(lefts.all(), w)
    for t in range(own):
        got = lax.dot_general(left, wide_right(source.get(t), w, 1), CONTRACT_LAST, preferred_element_type=F32)
        high, low = halves(got)
        for k in range(2 * terms):
            u_pair[k, t * n:(t + 1) * n, :w] = high[k * n:(k + 1) * n]
            u_pair[k, t * n:(t + 1) * n, w:] = low[k * n:(k + 1) * n]

    unroll = 8 if terms % 8 == 0 else 1

    def second_stage(i, carry):
        for j in range(unroll):
            k = i * unroll + j
            got = lax.dot_general(wide_left(u_pair[k], w), wide_right(right.get(k), w, 1), CONTRACT_LAST,
                                  preferred_element_type=F32)
            for t in range(own):
                total[inverse[k, first_own + t]] += got[t * n:(t + 1) * n]
            got = lax.dot_general(wide_left(u_pair[terms + k], w), wide_right(right.get(k), w, 0), CONTRACT_FIRST,
                                  preferred_element_type=F32)
            for t in range(own):
                total[tables[k, first_own + t]] += got[t * n:(t + 1) * n]
        return carry

    lax.fori_loop(0, terms // unroll, second_stage, 0)


def hand_out(plan, offsets, total, tables, rows_are, keep, send):
    side, mine, my_sec, my_rep = places(plan)
    rows = plan.rows
    row_id = lax.broadcasted_iota(jnp.int32, (rows, plan.width), 0)
    col_id = lax.broadcasted_iota(jnp.int32, (rows, plan.width), 1)
    for sec_off in range(plan.sec):
        for i, op_off in enumerate(offsets):
            for rep_off in range(plan.rep):
                inner = pl.multiple_of(lax.rem(my_rep + rep_off, plan.rep) * rows, rows)
                first_row = side * plan.part + lax.rem(mine + op_off, plan.half) * plan.block + inner
                goal = send if rep_off else keep
                for t in range(plan.own):
                    s = lax.rem(my_sec + sec_off, plan.sec) * plan.own + t
                    ok = row_id + first_row < tables[plan.terms + rows_are, s]
                    ok = ok & (col_id < tables[plan.terms + 1 - rows_are, s])
                    value = total[s, pl.ds(pl.multiple_of(i * plan.block + inner, rows), rows), :]
                    goal[sec_off, i, t * rows:(t + 1) * rows] = jnp.where(ok, value, 0.0)


def masked_wave(plan, tables, wave, t):
    rows, cols = lax.axis_index("sec") * plan.own + t, plan.terms
    row_id = lax.broadcasted_iota(jnp.int32, wave.shape[1:], 0)
    col_id = lax.broadcasted_iota(jnp.int32, wave.shape[1:], 1)
    ok = (row_id < tables[cols, rows]) & (col_id < tables[cols + 1, rows])
    return jnp.where(ok, wave[t], 0.0)


def first_kernel(plan, tables, wave, left_ops, right_ops,
                 keep, send, pieces, packed,
                 wave_in, left_in, right_in, flipped, a_away, u_pair, total, inverse, sems):
    side, mine, _, my_rep = places(plan)
    loads = ((wave, wave_in), (right_ops, right_in), (left_ops, left_in))
    copies = [pltpu.make_async_copy(src, dst, sems.at[i]) for i, (src, dst) in enumerate(loads)]
    for copy in copies:
        copy.start()
    home, right, source = stacks(plan, packed, "home", "right", "source")
    away, = stacks(plan, a_away, "away")
    half_at = pl.multiple_of(side * plan.part, plan.part)
    copies[0].wait()
    for t in range(plan.own):
        masked = masked_wave(plan, tables, wave_in, t)
        source.put(t, masked)
        wave_in[t] = masked
    for t in range(plan.own):
        flipped[t] = wave_in[t, :, pl.ds(half_at, plan.part)].T
        for off in range(plan.half):
            at = (lax.rem(mine + off, plan.half) * plan.rep + my_rep) * plan.rows
            value = flipped[t, pl.ds(pl.multiple_of(at, plan.rows), plan.rows), :]
            pieces[off, t * plan.rows:(t + 1) * plan.rows] = value
    copies[1].wait()
    prepare_left(plan, right_in, flipped.at[pl.ds(plan.own, plan.terms)], away, home)
    copies[2].wait()
    prepare_right(plan, left_in, right)
    apply_terms(plan, tables, inverse, away, right, source, u_pair, total)
    hand_out(plan, range(1, plan.half), total, tables, 1, keep, send)


def home_kernel(rows_are, names, plan, tables, *refs):
    packs, (keep, send, u_pair, total, inverse) = refs[:len(names)], refs[len(names):]
    home, right, source = [found for pack, part in zip(packs, names) for found in stacks(plan, pack, *part)]
    apply_terms(plan, tables, inverse, home, right, source, u_pair, total)
    hand_out(plan, range(1), total, tables, rows_are, keep, send)


def prepare_kernel(plan, tables, wave, left_ops, right_ops, a_away, packed, turned, flipped):
    home, right = stacks(plan, packed, "home", "right")
    away, = stacks(plan, a_away, "away")
    for t in range(plan.own):
        turned[t] = masked_wave(plan, tables, wave, t).T
    prepare_left(plan, left_ops, flipped, away, home)
    prepare_right(plan, right_ops, right)


def second_kernel(plan, tables, turned, a_away, packed, *rest):
    units, rest = rest[:2 * plan.op], rest[2 * plan.op:]
    (keep, send, s_pair, residual, norm, full, flipped, u_pair, total, inverse) = rest
    _, right = stacks(plan, packed, "home", "right")
    away, = stacks(plan, a_away, "away")
    source, = stacks(plan, s_pair, "source")
    side, mine, _, my_rep = places(plan)
    my_op = lax.axis_index("op")
    w, rows = plan.width, plan.rows
    sums = jnp.zeros((TILE, w), F32)
    for whose in range(2):
        for bits in range(plan.op):
            unit = units[whose * plan.op + bits]
            r = my_rep if whose == 0 else 1 - my_rep
            at = pl.multiple_of(((my_op ^ bits) * plan.rep + r) * rows, rows)
            for t in range(plan.own):
                full[t, pl.ds(at, rows), :] = unit[t * rows:(t + 1) * rows]
            sums = sums + unit[plan.piece:]
    entries = plan.sectors * w * w
    sums = jnp.broadcast_to(jnp.sum(sums, axis=1, keepdims=True), sums.shape)
    energy = sums[0:1] / sums[1:2]
    height = 1.0 + jnp.sqrt(sums[2:3] / entries) / TINY
    level = 1.0 / height
    at = pl.multiple_of((mine * plan.rep + my_rep) * rows, rows)
    half_at = pl.multiple_of(side * plan.part, plan.part)
    squares = jnp.zeros((8, w), F32)
    for t in range(plan.own):
        res = full[t] - energy * turned[t]
        squares = squares + jnp.sum((res * res).reshape(w // 8, 8, w), axis=0)
        full[t] = res
        source.put(t, res * level)
    for t in range(plan.own):
        flipped[t] = full[t, :, pl.ds(half_at, plan.part)].T
        residual[t] = flipped[t, pl.ds(at, rows), :]
    norm[0:4] = jnp.full((4, w), jnp.sum(squares), F32)
    norm[4:8] = jnp.broadcast_to(height, (4, w))
    apply_terms(plan, tables, inverse, away, right, source, u_pair, total)
    hand_out(plan, range(1, plan.half), total, tables, 0, keep, send)


def join_kernel(plan, sigma, extra, cross, unit):
    unit[:plan.piece] = sigma[...]
    row = lax.broadcasted_iota(jnp.int32, extra.shape, 0)
    unit[plan.piece:] = extra[...] + jnp.where(row == 0, cross[...], 0.0)


def sums_tile(products, squares, shares):
    rows = [sum(jnp.sum(x, axis=0, keepdims=True) for x in part) for part in (products, squares, shares)]
    return jnp.concatenate(rows + [jnp.zeros((TILE - 3,) + rows[0].shape[1:], F32)])


def gather_along_op(plan, piece, beside):
    if plan.op == 4:
        far = plan.flip_op(piece, 3)
        near = plan.flip_op(piece, 1)
        op = lax.axis_index("op")
        far, beside = lax.optimization_barrier((far, beside))
        carried = jnp.where((op == 1) | (op == 2), far, piece)
        return [piece, near, plan.onward(carried), far], beside
    got = piece[None]
    for bits in powers(plan.op):
        got = jnp.concatenate([got, plan.flip_op(got, bits)])
    return [got[i] for i in range(plan.op)], beside


def on_device(mesh_shape, wavefunction, left_operators, right_operators, coupling, left_sizes, right_sizes):
    plan = Plan(mesh_shape, wavefunction, left_operators, coupling)
    own, w, rows, terms = plan.own, plan.width, plan.rows, plan.terms
    smem = pl.BlockSpec(memory_space=pltpu.SMEM)
    vmem = pl.BlockSpec(memory_space=pltpu.VMEM)
    hbm = pl.BlockSpec(memory_space=pltpu.HBM)

    def spread(offsets):
        return jax.ShapeDtypeStruct((plan.sec, offsets, plan.piece, w), F32)

    def work(n):
        return [
            pltpu.VMEM((2 * terms, own * n, 2 * w), BF16),
            pltpu.VMEM((plan.sectors, n, w), F32),
            pltpu.SMEM((terms, plan.sectors), jnp.int32),
        ]

    def call(body, n, out_shape, in_specs, scratch, grant=28):
        flops = 3 * 2 * 2 * 2 * terms * own * n * w * w
        return pl.pallas_call(
            functools.partial(body, plan),
            out_shape=out_shape,
            in_specs=in_specs,
            out_specs=(vmem,) * len(out_shape),
            scratch_shapes=scratch,
            compiler_params=pltpu.CompilerParams(vmem_limit_bytes=grant << 20),
            cost_estimate=pl.CostEstimate(flops=flops, bytes_accessed=4 << 20, transcendentals=0),
        )

    blocks = jax.ShapeDtypeStruct((own, w, w), F32)
    def packed(*names):
        return jax.ShapeDtypeStruct(stack_shape(plan, *names), BF16)

    chunks = jax.ShapeDtypeStruct((plan.half, plan.piece, w), F32)
    operators = pltpu.VMEM((terms, w, w), F32)
    turned_operators = pltpu.VMEM((terms, plan.part, w), F32)
    tables = jnp.concatenate([coupling, left_sizes[None], right_sizes[None]])

    def ring_in_half(parts, at):
        run = parts[at(plan.half - 2)]
        for i in range(plan.half - 3, -1, -1):
            run = plan.next_in_half(run) + parts[at(i)]
        return plan.next_in_half(run)

    def along_half(keep, send, rows_are, names, home_args):
        away = keep + plan.across_cores(send)
        away, home_args = lax.optimization_barrier((away, home_args))
        others = ring_in_half(away[1:], lambda i: (slice(None), i))
        kept = call(
            functools.partial(home_kernel, rows_are, names), plan.block, (spread(1),) * 2,
            [smem] + [vmem] * len(names), work(plan.block),
        )(tables, *home_args)
        sent, others, kept = lax.optimization_barrier((away[0], others, kept))
        home = (kept[0] + plan.across_cores(kept[1]))[:, 0]
        return others + home[1:], home[0], ring_in_half(sent, lambda i: i), sent

    def along_sec(others, ours, extra):
        if plan.sec == 2:
            got = plan.next_sec(jnp.concatenate([others[0], extra]))
            return ours + got[:plan.piece], extra + got[plan.piece:], got[:plan.piece]
        run = others[plan.sec - 2]
        for i in range(plan.sec - 3, -1, -1):
            run = plan.next_sec(run) + others[i]
        run = plan.next_sec(run)
        for bits in powers(plan.sec):
            extra = extra + plan.flip_sec(extra, bits)
        return ours + run, extra, run

    keep, send, pieces, packs = call(
        first_kernel, plan.away,
        (spread(plan.half - 1),) * 2 + (chunks, packed("home", "right", "source")),
        [smem] + [hbm] * 3,
        [pltpu.VMEM(blocks.shape, F32), operators, operators, pltpu.VMEM((own + terms, plan.part, w), F32),
         pltpu.VMEM(packed("away").shape, BF16)] + work(plan.away) + [pltpu.SemaphoreType.DMA((3,))],
    )(tables, *[pltpu.with_memory_space_constraint(x, pltpu.HBM)
                for x in (wavefunction, left_operators, right_operators)])

    others, home, got, sent = along_half(keep, send, 1, (("home", "right", "source"),), (packs,))
    extra = sums_tile(
        [home * pieces[0]] + [sent[i] * pieces[1 + i] for i in range(plan.half - 1)], [pieces[0] ** 2],
        [(x * TINY) ** 2 for x in [home, *sent, *others]],
    )
    sigma, extra, crossed = along_sec(others, home + got, extra)
    cross = jnp.sum(crossed * pieces[0], axis=0, keepdims=True)
    if plan.sec == 2:
        cross = 2.0 * cross
    else:
        for bits in powers(plan.sec):
            cross = cross + plan.flip_sec(cross, bits)
    unit, = call(join_kernel, 1, (jax.ShapeDtypeStruct((plan.piece + TILE, w), F32),), [vmem] * 3, [])(
        sigma, extra, cross)

    unit, *again = lax.optimization_barrier((unit, wavefunction, left_operators, right_operators))
    prepared = call(
        prepare_kernel, 1, (packed("away"), packed("home", "right"), blocks), [smem] + [vmem] * 3, [turned_operators],
    )(tables, *again)
    units, (a_away, packs, turned) = gather_along_op(plan, unit, prepared)
    units = units + [plan.across_cores(x) for x in units]

    keep, send, s_pair, residual, norm = call(
        second_kernel, plan.away,
        (spread(plan.half - 1),) * 2 + (packed("source"), jax.ShapeDtypeStruct((own, rows, w), F32),
                                        jax.ShapeDtypeStruct((TILE, w), F32)),
        [smem] + [vmem] * (3 + len(units)),
        [pltpu.VMEM(blocks.shape, F32), pltpu.VMEM((own, plan.part, w), F32)] + work(plan.away),
    )(tables, turned, a_away, packs, *units)

    others, home, got, _ = along_half(keep, send, 0, (("home", "right"), ("source",)), (packs, s_pair))
    sigma, total, _ = along_sec(others, home + got, norm)
    entries = plan.sectors * w * w
    factor = norm[4:5] / jnp.sqrt(total[0:1] / entries + 1e-06)
    sigma_next = (sigma * factor).reshape(own, rows, w)
    return (sigma_next, residual)


def solution(mesh):
    in_specs = (
        P(("grp", "sec"), None, None),
        P(("op", "rep"), None, None),
        P(("op", "rep"), None, None),
        P(("op", "rep"), None),
        P("grp"),
        P("grp"),
    )
    out_specs = (P(("grp", "sec"), ("op", "rep"), None), P(("grp", "sec"), ("op", "rep"), None))
    return jax.shard_map(
        functools.partial(on_device, dict(mesh.shape)),
        mesh=mesh, in_specs=in_specs, out_specs=out_specs, check_vma=False,
    )
```

```python
import functools

import jax
import jax.numpy as jnp
from jax import lax
from jax.experimental import pallas as pl
from jax.experimental.pallas import tpu as pltpu
from jax.sharding import PartitionSpec as P

F32 = jnp.float32
BF16 = jnp.bfloat16
CONTRACT_LAST = (((1,), (1,)), ((), ()))
CONTRACT_FIRST = (((1,), (0,)), ((), ()))
EVERYONE = ("grp", "op", "sec", "rep")
TINY = 2.0 ** -32
TILE = 8


def halves(value):
    high = value.astype(BF16)
    low = (value - high.astype(F32)).astype(BF16)
    return high, low


def wide_left(pair, width):
    high, low = pair[:, :width], pair[:, width:]
    return jnp.concatenate([high, high, low], axis=1)


def wide_right(pair, width, axis):
    high, low = pair[:, :width], pair[:, width:]
    return jnp.concatenate([high, low, high], axis=axis)


def powers(count):
    return [1 << i for i in range(count.bit_length() - 1)]


class Plan:
    def __init__(self, mesh_shape, wavefunction, operators, coupling):
        self.grp, self.op, self.sec, self.rep = (mesh_shape[a] for a in EVERYONE)
        self.half = self.op // 2
        self.own, self.width = wavefunction.shape[0], wavefunction.shape[1]
        self.terms = operators.shape[0]
        self.sectors = coupling.shape[1]
        self.rows = self.width // (self.op * self.rep)
        self.block = self.rows * self.rep
        self.part = self.width // 2
        self.away = self.block * (self.half - 1)
        self.piece = self.own * self.rows

    def perm(self, move):
        def flat(g, o, s, r):
            return ((g * self.op + o) * self.sec + s) * self.rep + r

        pairs = []
        for g in range(self.grp):
            for o in range(self.op):
                for s in range(self.sec):
                    for r in range(self.rep):
                        pairs.append((flat(g, o, s, r), flat(g, *move(o, s, r))))
        return pairs

    def across_cores(self, x):
        return lax.ppermute(x, EVERYONE, self.perm(lambda o, s, r: (o, s, 1 - r)))

    def next_sec(self, x):
        return lax.ppermute(x, EVERYONE, self.perm(lambda o, s, r: (o, (s + 1) % self.sec, r)))

    def next_in_half(self, x):
        def move(o, s, r):
            base = o // self.half * self.half
            return (base + (o - base + 1) % self.half, s, r)

        return lax.ppermute(x, EVERYONE, self.perm(move))

    def flip_op(self, x, bits):
        return lax.ppermute(x, EVERYONE, self.perm(lambda o, s, r: (o ^ bits, s, r)))

    def flip_sec(self, x, bits):
        return lax.ppermute(x, EVERYONE, self.perm(lambda o, s, r: (o, s ^ bits, r)))

    def onward(self, x):
        to = {0: 2, 2: 3, 3: 1, 1: 0}
        return lax.ppermute(x, EVERYONE, self.perm(lambda o, s, r: (to[o], s, r)))


def places(plan):
    op = lax.axis_index("op")
    return lax.div(op, plan.half), lax.rem(op, plan.half), lax.axis_index("sec"), lax.axis_index("rep")


class Stack:
    def __init__(self, ref, start, count, height):
        self.ref, self.start, self.count, self.height = ref, start, count, height

    def span(self, block, rows=None):
        first, last = (0, self.height) if rows is None else rows
        return slice(self.start + block * self.height + first, self.start + block * self.height + last)

    def put(self, block, value, rows=None):
        width = value.shape[-1]
        at = self.span(block, rows)
        self.ref[at, :width], self.ref[at, width:] = halves(value)

    def get(self, block):
        if isinstance(block, int):
            return self.ref[self.span(block)]
        return self.ref[pl.ds(pl.multiple_of(self.start + block * self.height, 16), self.height)]

    def all(self):
        return self.ref[self.start:self.start + self.count * self.height]


def stacks(plan, ref, *names):
    sizes = dict(
        away=(2 * plan.terms, plan.away), home=(2 * plan.terms, plan.block),
        right=(plan.terms, plan.width), source=(plan.own, plan.width),
    )
    found, start = [], 0
    for name in names:
        count, height = sizes[name]
        found.append(Stack(ref, start, count, height))
        start += count * height
    return found


def stack_shape(plan, *names):
    end = stacks(plan, None, *names)[-1]
    return (end.start + end.count * end.height, 2 * plan.width)


def prepare_left(plan, left_in, flipped, away, home):
    side, mine, _, _ = places(plan)
    half_at = pl.multiple_of(side * plan.part, plan.part)
    for k in range(plan.terms):
        flipped[k] = left_in[k, :, pl.ds(half_at, plan.part)].T
    for off in range(plan.half):
        at = pl.multiple_of(lax.rem(mine + off, plan.half) * plan.block, plan.block)
        goal = away if off else home
        start = (off - 1) * plan.block if off else 0
        rows = (start, start + plan.block)
        for k in range(plan.terms):
            goal.put(k, left_in[k, pl.ds(pl.multiple_of(half_at + at, plan.block), plan.block), :], rows)
            goal.put(plan.terms + k, flipped[k, pl.ds(at, plan.block), :], rows)


def prepare_right(plan, right_in, right):
    for k in range(plan.terms):
        right.put(k, right_in[k])


def first_products(plan, lefts, source, u_pair):
    w, n = plan.width, lefts.height
    left = wide_left(lefts.all(), w)
    for t in range(plan.own):
        got = lax.dot_general(left, wide_right(source.get(t), w, 1), CONTRACT_LAST, preferred_element_type=F32)
        high, low = halves(got)
        for k in range(lefts.count):
            u_pair[k, t * n:(t + 1) * n, :w] = high[k * n:(k + 1) * n]
            u_pair[k, t * n:(t + 1) * n, w:] = low[k * n:(k + 1) * n]


def second_products(plan, tables, inverse, right, u_pair, total):
    w, terms, own, n = plan.width, plan.terms, plan.own, total.shape[1]
    first_own = lax.axis_index("sec") * own
    for k in range(terms):
        for s in range(plan.sectors):
            inverse[k, tables[k, s]] = s
    total[...] = jnp.zeros_like(total)

    def one_term(k, carry):
        got = lax.dot_general(wide_left(u_pair[k], w), wide_right(right.get(k), w, 1), CONTRACT_LAST,
                              preferred_element_type=F32)
        for t in range(own):
            total[inverse[k, first_own + t]] += got[t * n:(t + 1) * n]
        got = lax.dot_general(wide_left(u_pair[terms + k], w), wide_right(right.get(k), w, 0), CONTRACT_FIRST,
                              preferred_element_type=F32)
        for t in range(own):
            total[tables[k, first_own + t]] += got[t * n:(t + 1) * n]
        return carry

    if terms <= 8:
        for k in range(terms):
            one_term(k, 0)
    else:
        lax.fori_loop(0, terms, one_term, 0)


def apply_terms(plan, tables, inverse, lefts, right, source, u_pair, total):
    first_products(plan, lefts, source, u_pair)
    second_products(plan, tables, inverse, right, u_pair, total)


def hand_out(plan, offsets, total, tables, rows_are, keep, send):
    side, mine, my_sec, my_rep = places(plan)
    rows = plan.rows
    row_id = lax.broadcasted_iota(jnp.int32, (rows, plan.width), 0)
    col_id = lax.broadcasted_iota(jnp.int32, (rows, plan.width), 1)
    for sec_off in range(plan.sec):
        for i, op_off in enumerate(offsets):
            for rep_off in range(plan.rep):
                inner = pl.multiple_of(lax.rem(my_rep + rep_off, plan.rep) * rows, rows)
                first_row = side * plan.part + lax.rem(mine + op_off, plan.half) * plan.block + inner
                goal = send if rep_off else keep
                for t in range(plan.own):
                    s = lax.rem(my_sec + sec_off, plan.sec) * plan.own + t
                    ok = row_id + first_row < tables[plan.terms + rows_are, s]
                    ok = ok & (col_id < tables[plan.terms + 1 - rows_are, s])
                    value = total[s, pl.ds(pl.multiple_of(i * plan.block + inner, rows), rows), :]
                    goal[sec_off, i, t * rows:(t + 1) * rows] = jnp.where(ok, value, 0.0)


def masked_wave(plan, tables, wave, t):
    rows, cols = lax.axis_index("sec") * plan.own + t, plan.terms
    row_id = lax.broadcasted_iota(jnp.int32, wave.shape[1:], 0)
    col_id = lax.broadcasted_iota(jnp.int32, wave.shape[1:], 1)
    ok = (row_id < tables[cols, rows]) & (col_id < tables[cols + 1, rows])
    return jnp.where(ok, wave[t], 0.0)


class Tables:
    def __init__(self, coupling, *sizes):
        self.coupling, self.sizes, self.terms = coupling, sizes, coupling.shape[0]

    def __getitem__(self, at):
        row, sector = at
        if isinstance(row, int) and row >= self.terms:
            return self.sizes[row - self.terms][sector]
        return self.coupling[row, sector]


def first_kernel(plan, coupling, left_sizes, right_sizes, wave, left_ops, right_ops,
                 keep, send, pieces, packed,
                 wave_in, left_in, right_in, flipped, a_away, u_pair, total, inverse, sems):
    side, mine, _, my_rep = places(plan)
    tables = Tables(coupling, left_sizes, right_sizes)
    loads = ((wave, wave_in), (right_ops, right_in), (left_ops, left_in))
    copies = [pltpu.make_async_copy(src, dst, sems.at[i]) for i, (src, dst) in enumerate(loads)]
    for copy in copies:
        copy.start()
    home, right, source = stacks(plan, packed, "home", "right", "source")
    away, = stacks(plan, a_away, "away")
    half_at = pl.multiple_of(side * plan.part, plan.part)
    copies[0].wait()
    for t in range(plan.own):
        masked = masked_wave(plan, tables, wave_in, t)
        source.put(t, masked)
        wave_in[t] = masked
    for t in range(plan.own):
        flipped[t] = wave_in[t, :, pl.ds(half_at, plan.part)].T
        for off in range(plan.half):
            at = (lax.rem(mine + off, plan.half) * plan.rep + my_rep) * plan.rows
            value = flipped[t, pl.ds(pl.multiple_of(at, plan.rows), plan.rows), :]
            pieces[off, t * plan.rows:(t + 1) * plan.rows] = value
    copies[1].wait()
    prepare_left(plan, right_in, flipped.at[pl.ds(plan.own, plan.terms)], away, home)
    first_products(plan, away, source, u_pair)
    copies[2].wait()
    prepare_right(plan, left_in, right)
    second_products(plan, tables, inverse, right, u_pair, total)
    hand_out(plan, range(1, plan.half), total, tables, 1, keep, send)


def home_kernel(rows_are, names, plan, tables, *refs):
    packs, (keep, send, u_pair, total, inverse) = refs[:len(names)], refs[len(names):]
    home, right, source = [found for pack, part in zip(packs, names) for found in stacks(plan, pack, *part)]
    apply_terms(plan, tables, inverse, home, right, source, u_pair, total)
    hand_out(plan, range(1), total, tables, rows_are, keep, send)


def prepare_kernel(plan, tables, wave, left_ops, right_ops, a_away, packed, turned, flipped):
    home, right = stacks(plan, packed, "home", "right")
    away, = stacks(plan, a_away, "away")
    for t in range(plan.own):
        turned[t] = masked_wave(plan, tables, wave, t).T
    prepare_left(plan, left_ops, flipped, away, home)
    prepare_right(plan, right_ops, right)


def second_kernel(plan, tables, turned, a_away, packed, *rest):
    units, rest = rest[:2 * plan.op], rest[2 * plan.op:]
    (keep, send, s_pair, residual, norm, full, flipped, u_pair, total, inverse) = rest
    _, right = stacks(plan, packed, "home", "right")
    away, = stacks(plan, a_away, "away")
    source, = stacks(plan, s_pair, "source")
    side, mine, _, my_rep = places(plan)
    my_op = lax.axis_index("op")
    w, rows = plan.width, plan.rows
    sums = jnp.zeros((TILE, w), F32)
    for whose in range(2):
        for bits in range(plan.op):
            unit = units[whose * plan.op + bits]
            r = my_rep if whose == 0 else 1 - my_rep
            at = pl.multiple_of(((my_op ^ bits) * plan.rep + r) * rows, rows)
            for t in range(plan.own):
                full[t, pl.ds(at, rows), :] = unit[t * rows:(t + 1) * rows]
            sums = sums + unit[plan.piece:]
    entries = plan.sectors * w * w
    sums = jnp.broadcast_to(jnp.sum(sums, axis=1, keepdims=True), sums.shape)
    energy = sums[0:1] / sums[1:2]
    height = 1.0 + jnp.sqrt(sums[2:3] / entries) / TINY
    level = 1.0 / height
    at = pl.multiple_of((mine * plan.rep + my_rep) * rows, rows)
    half_at = pl.multiple_of(side * plan.part, plan.part)
    squares = jnp.zeros((8, w), F32)
    for t in range(plan.own):
        res = full[t] - energy * turned[t]
        squares = squares + jnp.sum((res * res).reshape(w // 8, 8, w), axis=0)
        full[t] = res
        source.put(t, res * level)
    for t in range(plan.own):
        flipped[t] = full[t, :, pl.ds(half_at, plan.part)].T
        residual[t] = flipped[t, pl.ds(at, rows), :]
    norm[0:4] = jnp.full((4, w), jnp.sum(squares), F32)
    norm[4:8] = jnp.broadcast_to(height, (4, w))
    apply_terms(plan, tables, inverse, away, right, source, u_pair, total)
    hand_out(plan, range(1, plan.half), total, tables, 0, keep, send)


def join_kernel(plan, sigma, extra, cross, unit):
    unit[:plan.piece] = sigma[...]
    row = lax.broadcasted_iota(jnp.int32, extra.shape, 0)
    unit[plan.piece:] = extra[...] + jnp.where(row == 0, cross[...], 0.0)


def sums_tile(products, squares, shares):
    rows = [sum(jnp.sum(x, axis=0, keepdims=True) for x in part) for part in (products, squares, shares)]
    return jnp.concatenate(rows + [jnp.zeros((TILE - 3,) + rows[0].shape[1:], F32)])


def gather_along_op(plan, piece, beside):
    if plan.op == 4:
        far = plan.flip_op(piece, 3)
        near = plan.flip_op(piece, 1)
        op = lax.axis_index("op")
        far, beside = lax.optimization_barrier((far, beside))
        carried = jnp.where((op == 1) | (op == 2), far, piece)
        return [piece, near, plan.onward(carried), far], beside
    got = piece[None]
    for bits in powers(plan.op):
        got = jnp.concatenate([got, plan.flip_op(got, bits)])
    return [got[i] for i in range(plan.op)], beside


def on_device(mesh_shape, wavefunction, left_operators, right_operators, coupling, left_sizes, right_sizes):
    plan = Plan(mesh_shape, wavefunction, left_operators, coupling)
    own, w, rows, terms = plan.own, plan.width, plan.rows, plan.terms
    smem = pl.BlockSpec(memory_space=pltpu.SMEM)
    vmem = pl.BlockSpec(memory_space=pltpu.VMEM)
    hbm = pl.BlockSpec(memory_space=pltpu.HBM)

    def spread(offsets):
        return jax.ShapeDtypeStruct((plan.sec, offsets, plan.piece, w), F32)

    def work(n):
        return [
            pltpu.VMEM((2 * terms, own * n, 2 * w), BF16),
            pltpu.VMEM((plan.sectors, n, w), F32),
            pltpu.SMEM((terms, plan.sectors), jnp.int32),
        ]

    def call(body, n, out_shape, in_specs, scratch, grant=28):
        flops = 3 * 2 * 2 * 2 * terms * own * n * w * w
        return pl.pallas_call(
            functools.partial(body, plan),
            out_shape=out_shape,
            in_specs=in_specs,
            out_specs=(vmem,) * len(out_shape),
            scratch_shapes=scratch,
            compiler_params=pltpu.CompilerParams(vmem_limit_bytes=grant << 20),
            cost_estimate=pl.CostEstimate(flops=flops, bytes_accessed=4 << 20, transcendentals=0),
        )

    blocks = jax.ShapeDtypeStruct((own, w, w), F32)
    def packed(*names):
        return jax.ShapeDtypeStruct(stack_shape(plan, *names), BF16)

    chunks = jax.ShapeDtypeStruct((plan.half, plan.piece, w), F32)
    operators = pltpu.VMEM((terms, w, w), F32)
    turned_operators = pltpu.VMEM((terms, plan.part, w), F32)

    def ring_in_half(parts, at):
        run = parts[at(plan.half - 2)]
        for i in range(plan.half - 3, -1, -1):
            run = plan.next_in_half(run) + parts[at(i)]
        return plan.next_in_half(run)

    def along_half(keep, send, rows_are, names, home_args, tables):
        away = keep + plan.across_cores(send)
        away, home_args = lax.optimization_barrier((away, home_args))
        others = ring_in_half(away[1:], lambda i: (slice(None), i))
        kept = call(
            functools.partial(home_kernel, rows_are, names), plan.block, (spread(1),) * 2,
            [smem] + [vmem] * len(names), work(plan.block),
        )(tables, *home_args)
        sent, others, kept = lax.optimization_barrier((away[0], others, kept))
        home = (kept[0] + plan.across_cores(kept[1]))[:, 0]
        return others + home[1:], home[0], ring_in_half(sent, lambda i: i), sent

    def along_sec(others, ours, extra):
        if plan.sec == 2:
            got = plan.next_sec(jnp.concatenate([others[0], extra]))
            return ours + got[:plan.piece], extra + got[plan.piece:], got[:plan.piece]
        run = others[plan.sec - 2]
        for i in range(plan.sec - 3, -1, -1):
            run = plan.next_sec(run) + others[i]
        run = plan.next_sec(run)
        for bits in powers(plan.sec):
            extra = extra + plan.flip_sec(extra, bits)
        return ours + run, extra, run

    keep, send, pieces, packs = call(
        first_kernel, plan.away,
        (spread(plan.half - 1),) * 2 + (chunks, packed("home", "right", "source")),
        [smem] * 3 + [hbm] * 3,
        [pltpu.VMEM(blocks.shape, F32), operators, operators, pltpu.VMEM((own + terms, plan.part, w), F32),
         pltpu.VMEM(packed("away").shape, BF16)] + work(plan.away) + [pltpu.SemaphoreType.DMA((3,))],
    )(*[pltpu.with_memory_space_constraint(x, pltpu.HBM)
        for x in (coupling, left_sizes, right_sizes, wavefunction, left_operators, right_operators)])
    keep, *again = lax.optimization_barrier((keep, coupling, left_sizes, right_sizes))
    tables = jnp.concatenate([again[0], again[1][None], again[2][None]])

    others, home, got, sent = along_half(keep, send, 1, (("home", "right", "source"),), (packs,), tables)
    extra = sums_tile(
        [home * pieces[0]] + [sent[i] * pieces[1 + i] for i in range(plan.half - 1)], [pieces[0] ** 2],
        [(x * TINY) ** 2 for x in [home, *sent, *others]],
    )
    sigma, extra, crossed = along_sec(others, home + got, extra)
    cross = jnp.sum(crossed * pieces[0], axis=0, keepdims=True)
    if plan.sec == 2:
        cross = 2.0 * cross
    else:
        for bits in powers(plan.sec):
            cross = cross + plan.flip_sec(cross, bits)
    unit, = call(join_kernel, 1, (jax.ShapeDtypeStruct((plan.piece + TILE, w), F32),), [vmem] * 3, [])(
        sigma, extra, cross)

    unit, *again = lax.optimization_barrier((unit, wavefunction, left_operators, right_operators))
    prepared = call(
        prepare_kernel, 1, (packed("away"), packed("home", "right"), blocks), [smem] + [vmem] * 3, [turned_operators],
    )(tables, *again)
    units, (a_away, packs, turned) = gather_along_op(plan, unit, prepared)
    units = units + [plan.across_cores(x) for x in units]

    keep, send, s_pair, residual, norm = call(
        second_kernel, plan.away,
        (spread(plan.half - 1),) * 2 + (packed("source"), jax.ShapeDtypeStruct((own, rows, w), F32),
                                        jax.ShapeDtypeStruct((TILE, w), F32)),
        [smem] + [vmem] * (3 + len(units)),
        [pltpu.VMEM(blocks.shape, F32), pltpu.VMEM((own, plan.part, w), F32)] + work(plan.away),
    )(tables, turned, a_away, packs, *units)

    others, home, got, _ = along_half(keep, send, 0, (("home", "right"), ("source",)), (packs, s_pair), tables)
    sigma, total, _ = along_sec(others, home + got, norm)
    entries = plan.sectors * w * w
    factor = norm[4:5] / jnp.sqrt(total[0:1] / entries + 1e-06)
    sigma_next = (sigma * factor).reshape(own, rows, w)
    return (sigma_next, residual)


def solution(mesh):
    in_specs = (
        P(("grp", "sec"), None, None),
        P(("op", "rep"), None, None),
        P(("op", "rep"), None, None),
        P(("op", "rep"), None),
        P("grp"),
        P("grp"),
    )
    out_specs = (P(("grp", "sec"), ("op", "rep"), None), P(("grp", "sec"), ("op", "rep"), None))
    return jax.shard_map(
        functools.partial(on_device, dict(mesh.shape)),
        mesh=mesh, in_specs=in_specs, out_specs=out_specs, check_vma=False,
    )
```

```python
import functools

import jax
import jax.numpy as jnp
from jax import lax
from jax.experimental import pallas as pl
from jax.experimental.pallas import tpu as pltpu
from jax.sharding import PartitionSpec as P

F32 = jnp.float32
BF16 = jnp.bfloat16
CONTRACT_LAST = (((1,), (1,)), ((), ()))
CONTRACT_FIRST = (((1,), (0,)), ((), ()))
EVERYONE = ("grp", "op", "sec", "rep")
TINY = 2.0 ** -32
TILE = 8


def halves(value):
    high = value.astype(BF16)
    low = (value - high.astype(F32)).astype(BF16)
    return high, low


def wide_left(pair, width):
    high, low = pair[:, :width], pair[:, width:]
    return jnp.concatenate([high, high, low], axis=1)


def wide_right(pair, width, axis):
    high, low = pair[:, :width], pair[:, width:]
    return jnp.concatenate([high, low, high], axis=axis)


def powers(count):
    return [1 << i for i in range(count.bit_length() - 1)]


class Plan:
    def __init__(self, mesh_shape, wavefunction, operators, coupling):
        self.grp, self.op, self.sec, self.rep = (mesh_shape[a] for a in EVERYONE)
        self.half = self.op // 2
        self.own, self.width = wavefunction.shape[0], wavefunction.shape[1]
        self.terms = operators.shape[0]
        self.sectors = coupling.shape[1]
        self.rows = self.width // (self.op * self.rep)
        self.block = self.rows * self.rep
        self.part = self.width // 2
        self.away = self.block * (self.half - 1)
        self.piece = self.own * self.rows

    def perm(self, move):
        def flat(g, o, s, r):
            return ((g * self.op + o) * self.sec + s) * self.rep + r

        pairs = []
        for g in range(self.grp):
            for o in range(self.op):
                for s in range(self.sec):
                    for r in range(self.rep):
                        pairs.append((flat(g, o, s, r), flat(g, *move(o, s, r))))
        return pairs

    def across_cores(self, x):
        return lax.ppermute(x, EVERYONE, self.perm(lambda o, s, r: (o, s, 1 - r)))

    def next_sec(self, x):
        return lax.ppermute(x, EVERYONE, self.perm(lambda o, s, r: (o, (s + 1) % self.sec, r)))

    def next_in_half(self, x):
        def move(o, s, r):
            base = o // self.half * self.half
            return (base + (o - base + 1) % self.half, s, r)

        return lax.ppermute(x, EVERYONE, self.perm(move))

    def flip_op(self, x, bits):
        return lax.ppermute(x, EVERYONE, self.perm(lambda o, s, r: (o ^ bits, s, r)))

    def flip_sec(self, x, bits):
        return lax.ppermute(x, EVERYONE, self.perm(lambda o, s, r: (o, s ^ bits, r)))

    def onward(self, x):
        to = {0: 2, 2: 3, 3: 1, 1: 0}
        return lax.ppermute(x, EVERYONE, self.perm(lambda o, s, r: (to[o], s, r)))


def places(plan):
    op = lax.axis_index("op")
    return lax.div(op, plan.half), lax.rem(op, plan.half), lax.axis_index("sec"), lax.axis_index("rep")


class Stack:
    def __init__(self, ref, start, count, height):
        self.ref, self.start, self.count, self.height = ref, start, count, height

    def span(self, block, rows=None):
        first, last = (0, self.height) if rows is None else rows
        return slice(self.start + block * self.height + first, self.start + block * self.height + last)

    def put(self, block, value, rows=None):
        width = value.shape[-1]
        at = self.span(block, rows)
        self.ref[at, :width], self.ref[at, width:] = halves(value)

    def get(self, block):
        if isinstance(block, int):
            return self.ref[self.span(block)]
        return self.ref[pl.ds(pl.multiple_of(self.start + block * self.height, 16), self.height)]

    def all(self):
        return self.ref[self.start:self.start + self.count * self.height]


def stacks(plan, ref, *names):
    sizes = dict(
        away=(2 * plan.terms, plan.away), home=(2 * plan.terms, plan.block),
        right=(plan.terms, plan.width), source=(plan.own, plan.width),
    )
    found, start = [], 0
    for name in names:
        count, height = sizes[name]
        found.append(Stack(ref, start, count, height))
        start += count * height
    return found


def stack_shape(plan, *names):
    end = stacks(plan, None, *names)[-1]
    return (end.start + end.count * end.height, 2 * plan.width)


def prepare_left(plan, left_in, flipped, away, home):
    side, mine, _, _ = places(plan)
    half_at = pl.multiple_of(side * plan.part, plan.part)
    for k in range(plan.terms):
        flipped[k] = left_in[k, :, pl.ds(half_at, plan.part)].T
    for off in range(plan.half):
        at = pl.multiple_of(lax.rem(mine + off, plan.half) * plan.block, plan.block)
        goal = away if off else home
        start = (off - 1) * plan.block if off else 0
        rows = (start, start + plan.block)
        for k in range(plan.terms):
            goal.put(k, left_in[k, pl.ds(pl.multiple_of(half_at + at, plan.block), plan.block), :], rows)
            goal.put(plan.terms + k, flipped[k, pl.ds(at, plan.block), :], rows)


def prepare_right(plan, right_in, right):
    for k in range(plan.terms):
        right.put(k, right_in[k])


def first_products(plan, lefts, source, u_pair):
    w, n = plan.width, lefts.height
    left = wide_left(lefts.all(), w)
    for t in range(plan.own):
        got = lax.dot_general(left, wide_right(source.get(t), w, 1), CONTRACT_LAST, preferred_element_type=F32)
        high, low = halves(got)
        for k in range(lefts.count):
            u_pair[k, t * n:(t + 1) * n, :w] = high[k * n:(k + 1) * n]
            u_pair[k, t * n:(t + 1) * n, w:] = low[k * n:(k + 1) * n]


def second_products(plan, tables, inverse, right, u_pair, total):
    w, terms, own, n = plan.width, plan.terms, plan.own, total.shape[1]
    first_own = lax.axis_index("sec") * own
    for k in range(terms):
        for s in range(plan.sectors):
            inverse[k, tables[k, s]] = s
    total[...] = jnp.zeros_like(total)

    def one_term(k, carry):
        got = lax.dot_general(wide_left(u_pair[k], w), wide_right(right.get(k), w, 1), CONTRACT_LAST,
                              preferred_element_type=F32)
        for t in range(own):
            total[inverse[k, first_own + t]] += got[t * n:(t + 1) * n]
        got = lax.dot_general(wide_left(u_pair[terms + k], w), wide_right(right.get(k), w, 0), CONTRACT_FIRST,
                              preferred_element_type=F32)
        for t in range(own):
            total[tables[k, first_own + t]] += got[t * n:(t + 1) * n]
        return carry

    if terms <= 8:
        for k in range(terms):
            one_term(k, 0)
    else:
        lax.fori_loop(0, terms, one_term, 0)


def apply_terms(plan, tables, inverse, lefts, right, source, u_pair, total):
    first_products(plan, lefts, source, u_pair)
    second_products(plan, tables, inverse, right, u_pair, total)


def hand_out(plan, offsets, total, tables, rows_are, keep, send_others, send_ours):
    side, mine, my_sec, my_rep = places(plan)
    rows = plan.rows
    row_id = lax.broadcasted_iota(jnp.int32, (rows, plan.width), 0)
    col_id = lax.broadcasted_iota(jnp.int32, (rows, plan.width), 1)
    for sec_off in range(plan.sec):
        for i, op_off in enumerate(offsets):
            for rep_off in range(plan.rep):
                inner = pl.multiple_of(lax.rem(my_rep + rep_off, plan.rep) * rows, rows)
                first_row = side * plan.part + lax.rem(mine + op_off, plan.half) * plan.block + inner
                if rep_off == 0:
                    goal = keep.at[sec_off, i]
                else:
                    goal = send_others.at[sec_off - 1, i] if sec_off else send_ours.at[i]
                for t in range(plan.own):
                    s = lax.rem(my_sec + sec_off, plan.sec) * plan.own + t
                    ok = row_id + first_row < tables[plan.terms + rows_are, s]
                    ok = ok & (col_id < tables[plan.terms + 1 - rows_are, s])
                    value = total[s, pl.ds(pl.multiple_of(i * plan.block + inner, rows), rows), :]
                    goal[t * rows:(t + 1) * rows] = jnp.where(ok, value, 0.0)


def masked_wave(plan, tables, wave, t):
    rows, cols = lax.axis_index("sec") * plan.own + t, plan.terms
    row_id = lax.broadcasted_iota(jnp.int32, wave.shape[1:], 0)
    col_id = lax.broadcasted_iota(jnp.int32, wave.shape[1:], 1)
    ok = (row_id < tables[cols, rows]) & (col_id < tables[cols + 1, rows])
    return jnp.where(ok, wave[t], 0.0)


class Tables:
    def __init__(self, coupling, *sizes):
        self.coupling, self.sizes, self.terms = coupling, sizes, coupling.shape[0]

    def __getitem__(self, at):
        row, sector = at
        if isinstance(row, int) and row >= self.terms:
            return self.sizes[row - self.terms][sector]
        return self.coupling[row, sector]


def first_kernel(plan, coupling_at, left_sizes_at, right_sizes_at, wave, left_ops, right_ops,
                 keep, send_others, send_ours, pieces, packed,
                 coupling, left_sizes, right_sizes, wave_in, left_in, right_in, flipped, a_away,
                 u_pair, total, inverse, sems):
    side, mine, _, my_rep = places(plan)
    tables = Tables(coupling, left_sizes, right_sizes)
    loads = ((wave, wave_in), (right_ops, right_in), (left_ops, left_in), (coupling_at, coupling),
             (left_sizes_at, left_sizes), (right_sizes_at, right_sizes))
    copies = [pltpu.make_async_copy(src, dst, sems.at[i]) for i, (src, dst) in enumerate(loads)]
    for copy in copies:
        copy.start()
    home, right, source = stacks(plan, packed, "home", "right", "source")
    away, = stacks(plan, a_away, "away")
    half_at = pl.multiple_of(side * plan.part, plan.part)
    for i in (3, 4, 5, 0):
        copies[i].wait()
    for t in range(plan.own):
        masked = masked_wave(plan, tables, wave_in, t)
        source.put(t, masked)
        wave_in[t] = masked
    for t in range(plan.own):
        flipped[t] = wave_in[t, :, pl.ds(half_at, plan.part)].T
        for off in range(plan.half):
            at = (lax.rem(mine + off, plan.half) * plan.rep + my_rep) * plan.rows
            value = flipped[t, pl.ds(pl.multiple_of(at, plan.rows), plan.rows), :]
            pieces[off, t * plan.rows:(t + 1) * plan.rows] = value
    copies[1].wait()
    prepare_left(plan, right_in, flipped.at[pl.ds(plan.own, plan.terms)], away, home)
    first_products(plan, away, source, u_pair)
    copies[2].wait()
    prepare_right(plan, left_in, right)
    second_products(plan, tables, inverse, right, u_pair, total)
    hand_out(plan, range(1, plan.half), total, tables, 1, keep, send_others, send_ours)


def home_kernel(rows_are, names, plan, tables, *refs):
    packs, refs = refs[:len(names)], refs[len(names):]
    keep, send_others, send_ours, u_pair, total, inverse = refs
    home, right, source = [found for pack, part in zip(packs, names) for found in stacks(plan, pack, *part)]
    apply_terms(plan, tables, inverse, home, right, source, u_pair, total)
    hand_out(plan, range(1), total, tables, rows_are, keep, send_others, send_ours)


def prepare_kernel(plan, tables, wave, left_ops, right_ops, a_away, packed, turned, flipped):
    home, right = stacks(plan, packed, "home", "right")
    away, = stacks(plan, a_away, "away")
    for t in range(plan.own):
        turned[t] = masked_wave(plan, tables, wave, t).T
    prepare_left(plan, left_ops, flipped, away, home)
    prepare_right(plan, right_ops, right)


def second_kernel(plan, tables, turned, a_away, packed, *rest):
    units, rest = rest[:2 * plan.op], rest[2 * plan.op:]
    (keep, send_others, send_ours, s_pair, full, norm, u_pair, total, inverse) = rest
    _, right = stacks(plan, packed, "home", "right")
    away, = stacks(plan, a_away, "away")
    source, = stacks(plan, s_pair, "source")
    my_op, my_rep = lax.axis_index("op"), lax.axis_index("rep")
    w, rows = plan.width, plan.rows
    sums = sum(unit[plan.piece:] for unit in units)
    entries = plan.sectors * w * w
    sums = jnp.broadcast_to(jnp.sum(sums, axis=1, keepdims=True), sums.shape)
    energy = sums[0:1] / sums[1:2]
    height = 1.0 + jnp.sqrt(sums[2:3] / entries) / TINY
    level = 1.0 / height
    squares = jnp.zeros((TILE, w), F32)
    for whose in range(2):
        r = my_rep if whose == 0 else 1 - my_rep
        for bits in range(plan.op):
            unit = units[whose * plan.op + bits]
            at = pl.multiple_of(((my_op ^ bits) * plan.rep + r) * rows, rows)
            for t in range(plan.own):
                res = unit[t * rows:(t + 1) * rows] - energy * turned[t, pl.ds(at, rows), :]
                squares = squares + jnp.sum(res.reshape(rows // TILE, TILE, w) ** 2, axis=0)
                full[t, pl.ds(at, rows), :] = res
    for t in range(plan.own):
        source.put(t, full[t] * level)
    norm[0:4] = jnp.full((4, w), jnp.sum(squares), F32)
    norm[4:8] = jnp.broadcast_to(height, (4, w))
    apply_terms(plan, tables, inverse, away, right, source, u_pair, total)
    hand_out(plan, range(1, plan.half), total, tables, 0, keep, send_others, send_ours)


def residual_kernel(plan, full, residual, flipped):
    side, mine, _, my_rep = places(plan)
    at = pl.multiple_of((mine * plan.rep + my_rep) * plan.rows, plan.rows)
    for t in range(plan.own):
        flipped[t] = full[t, :, pl.ds(pl.multiple_of(side * plan.part, plan.part), plan.part)].T
        residual[t] = flipped[t, pl.ds(at, plan.rows), :]


def join_kernel(plan, sigma, extra, cross, unit):
    unit[:plan.piece] = sigma[...]
    row = lax.broadcasted_iota(jnp.int32, extra.shape, 0)
    unit[plan.piece:] = extra[...] + jnp.where(row == 0, cross[...], 0.0)


def sums_tile(products, squares, shares):
    rows = [sum(jnp.sum(x, axis=0, keepdims=True) for x in part) for part in (products, squares, shares)]
    return jnp.concatenate(rows + [jnp.zeros((TILE - 3,) + rows[0].shape[1:], F32)])


def gather_along_op(plan, piece, beside):
    if plan.op == 4:
        far = plan.flip_op(piece, 3)
        near = plan.flip_op(piece, 1)
        op = lax.axis_index("op")
        far, beside = lax.optimization_barrier((far, beside))
        carried = jnp.where((op == 1) | (op == 2), far, piece)
        return [piece, near, plan.onward(carried), far], beside
    got = piece[None]
    for bits in powers(plan.op):
        got = jnp.concatenate([got, plan.flip_op(got, bits)])
    return [got[i] for i in range(plan.op)], beside


def on_device(mesh_shape, wavefunction, left_operators, right_operators, coupling, left_sizes, right_sizes):
    plan = Plan(mesh_shape, wavefunction, left_operators, coupling)
    own, w, rows, terms = plan.own, plan.width, plan.rows, plan.terms
    smem = pl.BlockSpec(memory_space=pltpu.SMEM)
    vmem = pl.BlockSpec(memory_space=pltpu.VMEM)
    hbm = pl.BlockSpec(memory_space=pltpu.HBM)

    def spread(offsets):
        shapes = ((plan.sec, offsets), (plan.sec - 1, offsets), (offsets,))
        return tuple(jax.ShapeDtypeStruct(x + (plan.piece, w), F32) for x in shapes)

    def work(n):
        return [
            pltpu.VMEM((2 * terms, own * n, 2 * w), BF16),
            pltpu.VMEM((plan.sectors, n, w), F32),
            pltpu.SMEM((terms, plan.sectors), jnp.int32),
        ]

    def call(body, n, out_shape, in_specs, scratch, grant=28):
        flops = 3 * 2 * 2 * 2 * terms * own * n * w * w
        return pl.pallas_call(
            functools.partial(body, plan),
            out_shape=out_shape,
            in_specs=in_specs,
            out_specs=(vmem,) * len(out_shape),
            scratch_shapes=scratch,
            compiler_params=pltpu.CompilerParams(vmem_limit_bytes=grant << 20),
            cost_estimate=pl.CostEstimate(flops=flops, bytes_accessed=4 << 20, transcendentals=0),
        )

    blocks = jax.ShapeDtypeStruct((own, w, w), F32)
    def packed(*names):
        return jax.ShapeDtypeStruct(stack_shape(plan, *names), BF16)

    chunks = jax.ShapeDtypeStruct((plan.half, plan.piece, w), F32)
    operators = pltpu.VMEM((terms, w, w), F32)
    turned_operators = pltpu.VMEM((terms, plan.part, w), F32)

    def ring_in_half(parts, at):
        run = parts[at(plan.half - 2)]
        for i in range(plan.half - 3, -1, -1):
            run = plan.next_in_half(run) + parts[at(i)]
        return plan.next_in_half(run)

    def along_half(sums, rows_are, names, home_args, tables):
        keep, send_others, send_ours = sums
        away = keep[1:] + plan.across_cores(send_others)
        away, home_args = lax.optimization_barrier((away, home_args))
        sent = keep[0] + plan.across_cores(send_ours)
        others = ring_in_half(away, lambda i: (slice(None), i))
        kept = call(
            functools.partial(home_kernel, rows_are, names), plan.block, spread(1),
            [smem] + [vmem] * len(names), work(plan.block),
        )(tables, *home_args)
        others, kept = lax.optimization_barrier((others, kept))
        keep, send_others, send_ours = kept
        others = others + (keep[1:] + plan.across_cores(send_others))[:, 0]
        home = (keep[0] + plan.across_cores(send_ours))[0]
        going, _ = lax.optimization_barrier((sent, keep))
        return others, home, ring_in_half(going, lambda i: i), sent

    def along_sec(others, ours, extra):
        if plan.sec == 2:
            got = plan.next_sec(jnp.concatenate([others[0], extra]))
            return ours + got[:plan.piece], extra + got[plan.piece:], got[:plan.piece]
        run = others[plan.sec - 2]
        for i in range(plan.sec - 3, -1, -1):
            run = plan.next_sec(run) + others[i]
        run = plan.next_sec(run)
        for bits in powers(plan.sec):
            extra = extra + plan.flip_sec(extra, bits)
        return ours + run, extra, run

    *sums, pieces, packs = call(
        first_kernel, plan.away,
        spread(plan.half - 1) + (chunks, packed("home", "right", "source")),
        [hbm] * 6,
        [pltpu.SMEM(x.shape, x.dtype) for x in (coupling, left_sizes, right_sizes)]
        + [pltpu.VMEM(blocks.shape, F32), operators, operators, pltpu.VMEM((own + terms, plan.part, w), F32),
         pltpu.VMEM(packed("away").shape, BF16)] + work(plan.away) + [pltpu.SemaphoreType.DMA((6,))],
    )(*[pltpu.with_memory_space_constraint(x, pltpu.HBM)
        for x in (coupling, left_sizes, right_sizes, wavefunction, left_operators, right_operators)])
    sums, *again = lax.optimization_barrier((sums, coupling, left_sizes, right_sizes))
    tables = jnp.concatenate([again[0], again[1][None], again[2][None]])

    others, home, got, sent = along_half(sums, 1, (("home", "right", "source"),), (packs,), tables)
    extra = sums_tile(
        [home * pieces[0]] + [sent[i] * pieces[1 + i] for i in range(plan.half - 1)], [pieces[0] ** 2],
        [(x * TINY) ** 2 for x in [home, *sent, *others]],
    )
    sigma, extra, crossed = along_sec(others, home + got, extra)
    cross = jnp.sum(crossed * pieces[0], axis=0, keepdims=True)
    if plan.sec == 2:
        cross = 2.0 * cross
    else:
        for bits in powers(plan.sec):
            cross = cross + plan.flip_sec(cross, bits)
    unit, = call(join_kernel, 1, (jax.ShapeDtypeStruct((plan.piece + TILE, w), F32),), [vmem] * 3, [])(
        sigma, extra, cross)

    unit, *again = lax.optimization_barrier((unit, wavefunction, left_operators, right_operators))
    prepared = call(
        prepare_kernel, 1, (packed("away"), packed("home", "right"), blocks), [smem] + [vmem] * 3, [turned_operators],
    )(tables, *again)
    units, (a_away, packs, turned) = gather_along_op(plan, unit, prepared)
    units = units + [plan.across_cores(x) for x in units]

    *sums, s_pair, full, norm = call(
        second_kernel, plan.away,
        spread(plan.half - 1) + (packed("source"), blocks, jax.ShapeDtypeStruct((TILE, w), F32)),
        [smem] + [vmem] * (3 + len(units)),
        work(plan.away),
    )(tables, turned, a_away, packs, *units)

    others, home, got, _ = along_half(sums, 0, (("home", "right"), ("source",)), (packs, s_pair), tables)
    residual, = call(residual_kernel, 1, (jax.ShapeDtypeStruct((own, rows, w), F32),), [vmem],
                     [pltpu.VMEM((own, plan.part, w), F32)])(full)
    sigma, total, _ = along_sec(others, home + got, norm)
    sigma, residual = lax.optimization_barrier((sigma, residual))
    entries = plan.sectors * w * w
    factor = norm[4:5] / jnp.sqrt(total[0:1] / entries + 1e-06)
    sigma_next = (sigma * factor).reshape(own, rows, w)
    return (sigma_next, residual)


def solution(mesh):
    in_specs = (
        P(("grp", "sec"), None, None),
        P(("op", "rep"), None, None),
        P(("op", "rep"), None, None),
        P(("op", "rep"), None),
        P("grp"),
        P("grp"),
    )
    out_specs = (P(("grp", "sec"), ("op", "rep"), None), P(("grp", "sec"), ("op", "rep"), None))
    return jax.shard_map(
        functools.partial(on_device, dict(mesh.shape)),
        mesh=mesh, in_specs=in_specs, out_specs=out_specs, check_vma=False,
    )
```

```python
import functools

import jax
import jax.numpy as jnp
from jax import lax
from jax.experimental import pallas as pl
from jax.experimental.pallas import tpu as pltpu
from jax.sharding import PartitionSpec as P

F32 = jnp.float32
BF16 = jnp.bfloat16
CONTRACT_LAST = (((1,), (1,)), ((), ()))
CONTRACT_FIRST = (((1,), (0,)), ((), ()))
EVERYONE = ("grp", "op", "sec", "rep")
TINY = 2.0 ** -32
TILE = 8


def halves(value):
    high = value.astype(BF16)
    low = (value - high.astype(F32)).astype(BF16)
    return high, low


def wide_left(pair, width):
    high, low = pair[:, :width], pair[:, width:]
    return jnp.concatenate([high, high, low], axis=1)


def wide_right(pair, width, axis):
    high, low = pair[:, :width], pair[:, width:]
    return jnp.concatenate([high, low, high], axis=axis)


def powers(count):
    return [1 << i for i in range(count.bit_length() - 1)]


class Plan:
    def __init__(self, mesh_shape, wavefunction, operators, coupling):
        self.grp, self.op, self.sec, self.rep = (mesh_shape[a] for a in EVERYONE)
        self.half = self.op // 2
        self.own, self.width = wavefunction.shape[0], wavefunction.shape[1]
        self.terms = operators.shape[0]
        self.sectors = coupling.shape[1]
        self.rows = self.width // (self.op * self.rep)
        self.block = self.rows * self.rep
        self.part = self.width // 2
        self.away = self.block * (self.half - 1)
        self.piece = self.own * self.rows

    def perm(self, move):
        def flat(g, o, s, r):
            return ((g * self.op + o) * self.sec + s) * self.rep + r

        pairs = []
        for g in range(self.grp):
            for o in range(self.op):
                for s in range(self.sec):
                    for r in range(self.rep):
                        pairs.append((flat(g, o, s, r), flat(g, *move(o, s, r))))
        return pairs

    def across_cores(self, x):
        return lax.ppermute(x, EVERYONE, self.perm(lambda o, s, r: (o, s, 1 - r)))

    def next_sec(self, x):
        return lax.ppermute(x, EVERYONE, self.perm(lambda o, s, r: (o, (s + 1) % self.sec, r)))

    def next_in_half(self, x):
        def move(o, s, r):
            base = o // self.half * self.half
            return (base + (o - base + 1) % self.half, s, r)

        return lax.ppermute(x, EVERYONE, self.perm(move))

    def flip_op(self, x, bits):
        return lax.ppermute(x, EVERYONE, self.perm(lambda o, s, r: (o ^ bits, s, r)))

    def flip_sec(self, x, bits):
        return lax.ppermute(x, EVERYONE, self.perm(lambda o, s, r: (o, s ^ bits, r)))


def places(plan):
    op = lax.axis_index("op")
    return lax.div(op, plan.half), lax.rem(op, plan.half), lax.axis_index("sec"), lax.axis_index("rep")


class Stack:
    def __init__(self, ref, start, count, height):
        self.ref, self.start, self.count, self.height = ref, start, count, height

    def span(self, block, rows=None):
        first, last = (0, self.height) if rows is None else rows
        return slice(self.start + block * self.height + first, self.start + block * self.height + last)

    def put(self, block, value, rows=None):
        width = value.shape[-1]
        at = self.span(block, rows)
        self.ref[at, :width], self.ref[at, width:] = halves(value)

    def get(self, block):
        if isinstance(block, int):
            return self.ref[self.span(block)]
        return self.ref[pl.ds(pl.multiple_of(self.start + block * self.height, 16), self.height)]

    def all(self):
        return self.ref[self.start:self.start + self.count * self.height]


def stacks(plan, ref, *names):
    sizes = dict(
        away=(2 * plan.terms, plan.away), home=(2 * plan.terms, plan.block),
        right=(plan.terms, plan.width), source=(plan.own, plan.width),
    )
    found, start = [], 0
    for name in names:
        count, height = sizes[name]
        found.append(Stack(ref, start, count, height))
        start += count * height
    return found


def stack_shape(plan, *names):
    end = stacks(plan, None, *names)[-1]
    return (end.start + end.count * end.height, 2 * plan.width)


def prepare_left(plan, left_in, flipped, away, home):
    side, mine, _, _ = places(plan)
    half_at = pl.multiple_of(side * plan.part, plan.part)
    for k in range(plan.terms):
        flipped[k] = left_in[k, :, pl.ds(half_at, plan.part)].T
    for off in range(plan.half):
        at = pl.multiple_of(lax.rem(mine + off, plan.half) * plan.block, plan.block)
        goal = away if off else home
        start = (off - 1) * plan.block if off else 0
        rows = (start, start + plan.block)
        for k in range(plan.terms):
            goal.put(k, left_in[k, pl.ds(pl.multiple_of(half_at + at, plan.block), plan.block), :], rows)
            goal.put(plan.terms + k, flipped[k, pl.ds(at, plan.block), :], rows)


def prepare_right(plan, right_in, right):
    for k in range(plan.terms):
        right.put(k, right_in[k])


def first_products(plan, lefts, source, u_pair):
    w, n = plan.width, lefts.height
    left = wide_left(lefts.all(), w)
    for t in range(plan.own):
        got = lax.dot_general(left, wide_right(source.get(t), w, 1), CONTRACT_LAST, preferred_element_type=F32)
        high, low = halves(got)
        for k in range(lefts.count):
            u_pair[k, t * n:(t + 1) * n, :w] = high[k * n:(k + 1) * n]
            u_pair[k, t * n:(t + 1) * n, w:] = low[k * n:(k + 1) * n]


def second_products(plan, tables, inverse, right, u_pair, total):
    w, terms, own, n = plan.width, plan.terms, plan.own, total.shape[1]
    first_own = lax.axis_index("sec") * own
    for k in range(terms):
        for s in range(plan.sectors):
            inverse[k, tables[k, s]] = s
    total[...] = jnp.zeros_like(total)

    def one_term(k, carry):
        got = lax.dot_general(wide_left(u_pair[k], w), wide_right(right.get(k), w, 1), CONTRACT_LAST,
                              preferred_element_type=F32)
        for t in range(own):
            total[inverse[k, first_own + t]] += got[t * n:(t + 1) * n]
        got = lax.dot_general(wide_left(u_pair[terms + k], w), wide_right(right.get(k), w, 0), CONTRACT_FIRST,
                              preferred_element_type=F32)
        for t in range(own):
            total[tables[k, first_own + t]] += got[t * n:(t + 1) * n]
        return carry

    if terms <= 8:
        for k in range(terms):
            one_term(k, 0)
    else:
        lax.fori_loop(0, terms, one_term, 0)


def apply_terms(plan, tables, inverse, lefts, right, source, u_pair, total):
    first_products(plan, lefts, source, u_pair)
    second_products(plan, tables, inverse, right, u_pair, total)


def hand_out(plan, offsets, total, tables, rows_are, keep, send_others, send_ours):
    side, mine, my_sec, my_rep = places(plan)
    rows = plan.rows
    row_id = lax.broadcasted_iota(jnp.int32, (rows, plan.width), 0)
    col_id = lax.broadcasted_iota(jnp.int32, (rows, plan.width), 1)
    for sec_off in range(plan.sec):
        for i, op_off in enumerate(offsets):
            for rep_off in range(plan.rep):
                inner = pl.multiple_of(lax.rem(my_rep + rep_off, plan.rep) * rows, rows)
                first_row = side * plan.part + lax.rem(mine + op_off, plan.half) * plan.block + inner
                if rep_off == 0:
                    goal = keep.at[sec_off, i]
                else:
                    goal = send_others.at[sec_off - 1, i] if sec_off else send_ours.at[i]
                for t in range(plan.own):
                    s = lax.rem(my_sec + sec_off, plan.sec) * plan.own + t
                    ok = row_id + first_row < tables[plan.terms + rows_are, s]
                    ok = ok & (col_id < tables[plan.terms + 1 - rows_are, s])
                    value = total[s, pl.ds(pl.multiple_of(i * plan.block + inner, rows), rows), :]
                    goal[t * rows:(t + 1) * rows] = jnp.where(ok, value, 0.0)


def masked_wave(plan, tables, wave, t):
    rows, cols = lax.axis_index("sec") * plan.own + t, plan.terms
    row_id = lax.broadcasted_iota(jnp.int32, wave.shape[1:], 0)
    col_id = lax.broadcasted_iota(jnp.int32, wave.shape[1:], 1)
    ok = (row_id < tables[cols, rows]) & (col_id < tables[cols + 1, rows])
    return jnp.where(ok, wave[t], 0.0)


class Tables:
    def __init__(self, coupling, *sizes):
        self.coupling, self.sizes, self.terms = coupling, sizes, coupling.shape[0]

    def __getitem__(self, at):
        row, sector = at
        if isinstance(row, int) and row >= self.terms:
            return self.sizes[row - self.terms][sector]
        return self.coupling[row, sector]


def first_kernel(plan, coupling_at, left_sizes_at, right_sizes_at, wave, left_ops, right_ops,
                 keep, send_others, send_ours, pieces, packed,
                 coupling, left_sizes, right_sizes, wave_in, left_in, right_in, flipped, a_away,
                 u_pair, total, inverse, sems):
    side, mine, _, my_rep = places(plan)
    tables = Tables(coupling, left_sizes, right_sizes)
    loads = ((wave, wave_in), (right_ops, right_in), (left_ops, left_in), (coupling_at, coupling),
             (left_sizes_at, left_sizes), (right_sizes_at, right_sizes))
    copies = [pltpu.make_async_copy(src, dst, sems.at[i]) for i, (src, dst) in enumerate(loads)]
    for copy in copies:
        copy.start()
    home, right, source = stacks(plan, packed, "home", "right", "source")
    away, = stacks(plan, a_away, "away")
    half_at = pl.multiple_of(side * plan.part, plan.part)
    for i in (3, 4, 5, 0):
        copies[i].wait()
    for t in range(plan.own):
        masked = masked_wave(plan, tables, wave_in, t)
        source.put(t, masked)
        wave_in[t] = masked
    for t in range(plan.own):
        flipped[t] = wave_in[t, :, pl.ds(half_at, plan.part)].T
        for off in range(plan.half):
            at = (lax.rem(mine + off, plan.half) * plan.rep + my_rep) * plan.rows
            value = flipped[t, pl.ds(pl.multiple_of(at, plan.rows), plan.rows), :]
            pieces[off, t * plan.rows:(t + 1) * plan.rows] = value
    copies[1].wait()
    prepare_left(plan, right_in, flipped.at[pl.ds(plan.own, plan.terms)], away, home)
    first_products(plan, away, source, u_pair)
    copies[2].wait()
    prepare_right(plan, left_in, right)
    second_products(plan, tables, inverse, right, u_pair, total)
    hand_out(plan, range(1, plan.half), total, tables, 1, keep, send_others, send_ours)


def home_kernel(rows_are, names, plan, tables, *refs):
    packs, refs = refs[:len(names)], refs[len(names):]
    keep, send_others, send_ours, u_pair, total, inverse = refs
    home, right, source = [found for pack, part in zip(packs, names) for found in stacks(plan, pack, *part)]
    apply_terms(plan, tables, inverse, home, right, source, u_pair, total)
    hand_out(plan, range(1), total, tables, rows_are, keep, send_others, send_ours)


def prepare_kernel(plan, tables, wave, left_ops, right_ops, a_away, packed, turned, flipped):
    home, right = stacks(plan, packed, "home", "right")
    away, = stacks(plan, a_away, "away")
    for t in range(plan.own):
        turned[t] = masked_wave(plan, tables, wave, t).T
    prepare_left(plan, left_ops, flipped, away, home)
    prepare_right(plan, right_ops, right)


def second_kernel(plan, tables, turned, a_away, packed, *rest):
    units, rest = rest[:2 * plan.op], rest[2 * plan.op:]
    (keep, send_others, send_ours, s_pair, full, norm, u_pair, total, inverse) = rest
    _, right = stacks(plan, packed, "home", "right")
    away, = stacks(plan, a_away, "away")
    source, = stacks(plan, s_pair, "source")
    my_op, my_rep = lax.axis_index("op"), lax.axis_index("rep")
    w, rows = plan.width, plan.rows
    sums = sum(unit[plan.piece:] for unit in units)
    entries = plan.sectors * w * w
    sums = jnp.broadcast_to(jnp.sum(sums, axis=1, keepdims=True), sums.shape)
    energy = sums[0:1] / sums[1:2]
    height = 1.0 + jnp.sqrt(sums[2:3] / entries) / TINY
    level = 1.0 / height
    squares = jnp.zeros((TILE, w), F32)
    for whose in range(2):
        r = my_rep if whose == 0 else 1 - my_rep
        for bits in range(plan.op):
            unit = units[whose * plan.op + bits]
            at = pl.multiple_of(((my_op ^ bits) * plan.rep + r) * rows, rows)
            for t in range(plan.own):
                res = unit[t * rows:(t + 1) * rows] - energy * turned[t, pl.ds(at, rows), :]
                squares = squares + jnp.sum(res.reshape(rows // TILE, TILE, w) ** 2, axis=0)
                full[t, pl.ds(at, rows), :] = res
    for t in range(plan.own):
        source.put(t, full[t] * level)
    norm[0:4] = jnp.full((4, w), jnp.sum(squares), F32)
    norm[4:8] = jnp.broadcast_to(height, (4, w))
    apply_terms(plan, tables, inverse, away, right, source, u_pair, total)
    hand_out(plan, range(1, plan.half), total, tables, 0, keep, send_others, send_ours)


def residual_kernel(plan, full, residual, flipped):
    side, mine, _, my_rep = places(plan)
    at = pl.multiple_of((mine * plan.rep + my_rep) * plan.rows, plan.rows)
    for t in range(plan.own):
        flipped[t] = full[t, :, pl.ds(pl.multiple_of(side * plan.part, plan.part), plan.part)].T
        residual[t] = flipped[t, pl.ds(at, plan.rows), :]


def join_kernel(plan, sigma, extra, cross, unit):
    unit[:plan.piece] = sigma[...]
    row = lax.broadcasted_iota(jnp.int32, extra.shape, 0)
    unit[plan.piece:] = extra[...] + jnp.where(row == 0, cross[...], 0.0)


def sums_tile(products, squares, shares):
    rows = [sum(jnp.sum(x, axis=0, keepdims=True) for x in part) for part in (products, squares, shares)]
    return jnp.concatenate(rows + [jnp.zeros((TILE - 3,) + rows[0].shape[1:], F32)])


def gather_along_op(plan, piece, beside):
    if plan.op == 4:
        far = plan.flip_op(piece, 3)
        near = plan.flip_op(piece, 1)
        far, beside = lax.optimization_barrier((far, beside))
        return [piece, near, plan.flip_op(far, 1), far], beside
    got = piece[None]
    for bits in powers(plan.op):
        got = jnp.concatenate([got, plan.flip_op(got, bits)])
    return [got[i] for i in range(plan.op)], beside


def on_device(mesh_shape, wavefunction, left_operators, right_operators, coupling, left_sizes, right_sizes):
    plan = Plan(mesh_shape, wavefunction, left_operators, coupling)
    own, w, rows, terms = plan.own, plan.width, plan.rows, plan.terms
    smem = pl.BlockSpec(memory_space=pltpu.SMEM)
    vmem = pl.BlockSpec(memory_space=pltpu.VMEM)
    hbm = pl.BlockSpec(memory_space=pltpu.HBM)

    def spread(offsets):
        shapes = ((plan.sec, offsets), (plan.sec - 1, offsets), (offsets,))
        return tuple(jax.ShapeDtypeStruct(x + (plan.piece, w), F32) for x in shapes)

    def work(n):
        return [
            pltpu.VMEM((2 * terms, own * n, 2 * w), BF16),
            pltpu.VMEM((plan.sectors, n, w), F32),
            pltpu.SMEM((terms, plan.sectors), jnp.int32),
        ]

    def call(body, n, out_shape, in_specs, scratch, grant=28):
        flops = 3 * 2 * 2 * 2 * terms * own * n * w * w
        return pl.pallas_call(
            functools.partial(body, plan),
            out_shape=out_shape,
            in_specs=in_specs,
            out_specs=(vmem,) * len(out_shape),
            scratch_shapes=scratch,
            compiler_params=pltpu.CompilerParams(vmem_limit_bytes=grant << 20),
            cost_estimate=pl.CostEstimate(flops=flops, bytes_accessed=4 << 20, transcendentals=0),
        )

    blocks = jax.ShapeDtypeStruct((own, w, w), F32)
    def packed(*names):
        return jax.ShapeDtypeStruct(stack_shape(plan, *names), BF16)

    chunks = jax.ShapeDtypeStruct((plan.half, plan.piece, w), F32)
    operators = pltpu.VMEM((terms, w, w), F32)
    turned_operators = pltpu.VMEM((terms, plan.part, w), F32)

    def ring_in_half(parts, at):
        run = parts[at(plan.half - 2)]
        for i in range(plan.half - 3, -1, -1):
            run = plan.next_in_half(run) + parts[at(i)]
        return plan.next_in_half(run)

    def along_half(sums, rows_are, names, home_args, tables):
        keep, send_others, send_ours = sums
        away = keep[1:] + plan.across_cores(send_others)
        away, home_args = lax.optimization_barrier((away, home_args))
        sent = keep[0] + plan.across_cores(send_ours)
        others = ring_in_half(away, lambda i: (slice(None), i))
        kept = call(
            functools.partial(home_kernel, rows_are, names), plan.block, spread(1),
            [smem] + [vmem] * len(names), work(plan.block),
        )(tables, *home_args)
        others, kept = lax.optimization_barrier((others, kept))
        keep, send_others, send_ours = kept
        others = others + (keep[1:] + plan.across_cores(send_others))[:, 0]
        home = (keep[0] + plan.across_cores(send_ours))[0]
        going, _ = lax.optimization_barrier((sent, keep))
        return others, home, ring_in_half(going, lambda i: i), sent

    def along_sec(others, ours, extra):
        if plan.sec == 2:
            got = plan.next_sec(jnp.concatenate([others[0], extra]))
            return ours + got[:plan.piece], extra + got[plan.piece:], got[:plan.piece]
        run = others[plan.sec - 2]
        for i in range(plan.sec - 3, -1, -1):
            run = plan.next_sec(run) + others[i]
        run = plan.next_sec(run)
        for bits in powers(plan.sec):
            extra = extra + plan.flip_sec(extra, bits)
        return ours + run, extra, run

    *sums, pieces, packs = call(
        first_kernel, plan.away,
        spread(plan.half - 1) + (chunks, packed("home", "right", "source")),
        [hbm] * 6,
        [pltpu.SMEM(x.shape, x.dtype) for x in (coupling, left_sizes, right_sizes)]
        + [pltpu.VMEM(blocks.shape, F32), operators, operators, pltpu.VMEM((own + terms, plan.part, w), F32),
         pltpu.VMEM(packed("away").shape, BF16)] + work(plan.away) + [pltpu.SemaphoreType.DMA((6,))],
    )(*[pltpu.with_memory_space_constraint(x, pltpu.HBM)
        for x in (coupling, left_sizes, right_sizes, wavefunction, left_operators, right_operators)])
    sums, *again = lax.optimization_barrier((sums, coupling, left_sizes, right_sizes))
    tables = jnp.concatenate([again[0], again[1][None], again[2][None]])

    others, home, got, sent = along_half(sums, 1, (("home", "right", "source"),), (packs,), tables)
    extra = sums_tile(
        [home * pieces[0]] + [sent[i] * pieces[1 + i] for i in range(plan.half - 1)], [pieces[0] ** 2],
        [(x * TINY) ** 2 for x in [home, *sent, *others]],
    )
    sigma, extra, crossed = along_sec(others, home + got, extra)
    cross = jnp.sum(crossed * pieces[0], axis=0, keepdims=True)
    if plan.sec == 2:
        cross = 2.0 * cross
    else:
        for bits in powers(plan.sec):
            cross = cross + plan.flip_sec(cross, bits)
    unit, = call(join_kernel, 1, (jax.ShapeDtypeStruct((plan.piece + TILE, w), F32),), [vmem] * 3, [])(
        sigma, extra, cross)

    unit, *again = lax.optimization_barrier((unit, wavefunction, left_operators, right_operators))
    prepared = call(
        prepare_kernel, 1, (packed("away"), packed("home", "right"), blocks), [smem] + [vmem] * 3, [turned_operators],
    )(tables, *again)
    units, (a_away, packs, turned) = gather_along_op(plan, unit, prepared)
    units = units + [plan.across_cores(x) for x in units]

    *sums, s_pair, full, norm = call(
        second_kernel, plan.away,
        spread(plan.half - 1) + (packed("source"), blocks, jax.ShapeDtypeStruct((TILE, w), F32)),
        [smem] + [vmem] * (3 + len(units)),
        work(plan.away),
    )(tables, turned, a_away, packs, *units)

    others, home, got, _ = along_half(sums, 0, (("home", "right"), ("source",)), (packs, s_pair), tables)
    residual, = call(residual_kernel, 1, (jax.ShapeDtypeStruct((own, rows, w), F32),), [vmem],
                     [pltpu.VMEM((own, plan.part, w), F32)])(full)
    sigma, total, _ = along_sec(others, home + got, norm)
    sigma, residual = lax.optimization_barrier((sigma, residual))
    entries = plan.sectors * w * w
    factor = norm[4:5] / jnp.sqrt(total[0:1] / entries + 1e-06)
    sigma_next = (sigma * factor).reshape(own, rows, w)
    return (sigma_next, residual)


def solution(mesh):
    in_specs = (
        P(("grp", "sec"), None, None),
        P(("op", "rep"), None, None),
        P(("op", "rep"), None, None),
        P(("op", "rep"), None),
        P("grp"),
        P("grp"),
    )
    out_specs = (P(("grp", "sec"), ("op", "rep"), None), P(("grp", "sec"), ("op", "rep"), None))
    return jax.shard_map(
        functools.partial(on_device, dict(mesh.shape)),
        mesh=mesh, in_specs=in_specs, out_specs=out_specs, check_vma=False,
    )
```

```python
import functools

import jax
import jax.numpy as jnp
from jax import lax
from jax.experimental import pallas as pl
from jax.experimental.pallas import tpu as pltpu
from jax.sharding import PartitionSpec as P

F32 = jnp.float32
BF16 = jnp.bfloat16
CONTRACT_LAST = (((1,), (1,)), ((), ()))
CONTRACT_FIRST = (((1,), (0,)), ((), ()))
EVERYONE = ("grp", "op", "sec", "rep")
TINY = 2.0 ** -32
TILE = 8


def halves(value):
    high = value.astype(BF16)
    low = (value - high.astype(F32)).astype(BF16)
    return high, low


def wide_left(pair, width):
    high, low = pair[:, :width], pair[:, width:]
    return jnp.concatenate([high, high, low], axis=1)


def wide_right(pair, width, axis):
    high, low = pair[:, :width], pair[:, width:]
    return jnp.concatenate([high, low, high], axis=axis)


def powers(count):
    return [1 << i for i in range(count.bit_length() - 1)]


class Plan:
    def __init__(self, mesh_shape, wavefunction, operators, coupling):
        self.grp, self.op, self.sec, self.rep = (mesh_shape[a] for a in EVERYONE)
        self.half = self.op // 2
        self.own, self.width = wavefunction.shape[0], wavefunction.shape[1]
        self.terms = operators.shape[0]
        self.sectors = coupling.shape[1]
        self.rows = self.width // (self.op * self.rep)
        self.block = self.rows * self.rep
        self.part = self.width // 2
        self.away = self.block * (self.half - 1)
        self.piece = self.own * self.rows

    def perm(self, move):
        def flat(g, o, s, r):
            return ((g * self.op + o) * self.sec + s) * self.rep + r

        pairs = []
        for g in range(self.grp):
            for o in range(self.op):
                for s in range(self.sec):
                    for r in range(self.rep):
                        pairs.append((flat(g, o, s, r), flat(g, *move(o, s, r))))
        return pairs

    def across_cores(self, x):
        return lax.ppermute(x, EVERYONE, self.perm(lambda o, s, r: (o, s, 1 - r)))

    def next_sec(self, x):
        return lax.ppermute(x, EVERYONE, self.perm(lambda o, s, r: (o, (s + 1) % self.sec, r)))

    def next_in_half(self, x):
        def move(o, s, r):
            base = o // self.half * self.half
            return (base + (o - base + 1) % self.half, s, r)

        return lax.ppermute(x, EVERYONE, self.perm(move))

    def flip_op(self, x, bits):
        return lax.ppermute(x, EVERYONE, self.perm(lambda o, s, r: (o ^ bits, s, r)))

    def flip_sec(self, x, bits):
        return lax.ppermute(x, EVERYONE, self.perm(lambda o, s, r: (o, s ^ bits, r)))


def places(plan):
    op = lax.axis_index("op")
    return lax.div(op, plan.half), lax.rem(op, plan.half), lax.axis_index("sec"), lax.axis_index("rep")


class Stack:
    def __init__(self, ref, start, count, height):
        self.ref, self.start, self.count, self.height = ref, start, count, height

    def span(self, block, rows=None):
        first, last = (0, self.height) if rows is None else rows
        return slice(self.start + block * self.height + first, self.start + block * self.height + last)

    def put(self, block, value, rows=None):
        width = value.shape[-1]
        at = self.span(block, rows)
        self.ref[at, :width], self.ref[at, width:] = halves(value)

    def get(self, block):
        if isinstance(block, int):
            return self.ref[self.span(block)]
        return self.ref[pl.ds(pl.multiple_of(self.start + block * self.height, 16), self.height)]

    def all(self):
        return self.ref[self.start:self.start + self.count * self.height]


def stacks(plan, ref, *names):
    sizes = dict(
        away=(2 * plan.terms, plan.away), home=(2 * plan.terms, plan.block),
        right=(plan.terms, plan.width), source=(plan.own, plan.width),
    )
    found, start = [], 0
    for name in names:
        count, height = sizes[name]
        found.append(Stack(ref, start, count, height))
        start += count * height
    return found


def stack_shape(plan, *names):
    end = stacks(plan, None, *names)[-1]
    return (end.start + end.count * end.height, 2 * plan.width)


def prepare_left(plan, left_in, flipped, away, home):
    side, mine, _, _ = places(plan)
    half_at = pl.multiple_of(side * plan.part, plan.part)
    for k in range(plan.terms):
        flipped[k] = left_in[k, :, pl.ds(half_at, plan.part)].T
    for off in range(plan.half):
        at = pl.multiple_of(lax.rem(mine + off, plan.half) * plan.block, plan.block)
        goal = away if off else home
        start = (off - 1) * plan.block if off else 0
        rows = (start, start + plan.block)
        for k in range(plan.terms):
            goal.put(k, left_in[k, pl.ds(pl.multiple_of(half_at + at, plan.block), plan.block), :], rows)
            goal.put(plan.terms + k, flipped[k, pl.ds(at, plan.block), :], rows)


def prepare_right(plan, right_in, right):
    for k in range(plan.terms):
        right.put(k, right_in[k])


def first_products(plan, lefts, source, u_pair):
    w, n = plan.width, lefts.height
    left = wide_left(lefts.all(), w)
    for t in range(plan.own):
        got = lax.dot_general(left, wide_right(source.get(t), w, 1), CONTRACT_LAST, preferred_element_type=F32)
        high, low = halves(got)
        for k in range(lefts.count):
            u_pair[k, t * n:(t + 1) * n, :w] = high[k * n:(k + 1) * n]
            u_pair[k, t * n:(t + 1) * n, w:] = low[k * n:(k + 1) * n]


def second_products(plan, tables, inverse, right, u_pair, total):
    w, terms, own, n = plan.width, plan.terms, plan.own, total.shape[1]
    first_own = lax.axis_index("sec") * own
    for k in range(terms):
        for s in range(plan.sectors):
            inverse[k, tables[k, s]] = s
    total[...] = jnp.zeros_like(total)

    def one_term(k, carry):
        got = lax.dot_general(wide_left(u_pair[k], w), wide_right(right.get(k), w, 1), CONTRACT_LAST,
                              preferred_element_type=F32)
        for t in range(own):
            total[inverse[k, first_own + t]] += got[t * n:(t + 1) * n]
        got = lax.dot_general(wide_left(u_pair[terms + k], w), wide_right(right.get(k), w, 0), CONTRACT_FIRST,
                              preferred_element_type=F32)
        for t in range(own):
            total[tables[k, first_own + t]] += got[t * n:(t + 1) * n]
        return carry

    if terms <= 8:
        for k in range(terms):
            one_term(k, 0)
    else:
        lax.fori_loop(0, terms, one_term, 0)


def apply_terms(plan, tables, inverse, lefts, right, source, u_pair, total):
    first_products(plan, lefts, source, u_pair)
    second_products(plan, tables, inverse, right, u_pair, total)


def hand_out(plan, offsets, total, tables, rows_are, keep, send_others, send_ours):
    side, mine, my_sec, my_rep = places(plan)
    rows = plan.rows
    row_id = lax.broadcasted_iota(jnp.int32, (rows, plan.width), 0)
    col_id = lax.broadcasted_iota(jnp.int32, (rows, plan.width), 1)
    for sec_off in range(plan.sec):
        for i, op_off in enumerate(offsets):
            for rep_off in range(plan.rep):
                inner = pl.multiple_of(lax.rem(my_rep + rep_off, plan.rep) * rows, rows)
                first_row = side * plan.part + lax.rem(mine + op_off, plan.half) * plan.block + inner
                if rep_off == 0:
                    goal = keep.at[sec_off, i]
                else:
                    goal = send_others.at[sec_off - 1, i] if sec_off else send_ours.at[i]
                for t in range(plan.own):
                    s = lax.rem(my_sec + sec_off, plan.sec) * plan.own + t
                    ok = row_id + first_row < tables[plan.terms + rows_are, s]
                    ok = ok & (col_id < tables[plan.terms + 1 - rows_are, s])
                    value = total[s, pl.ds(pl.multiple_of(i * plan.block + inner, rows), rows), :]
                    goal[t * rows:(t + 1) * rows] = jnp.where(ok, value, 0.0)


def masked_wave(plan, tables, wave, t):
    rows, cols = lax.axis_index("sec") * plan.own + t, plan.terms
    row_id = lax.broadcasted_iota(jnp.int32, wave.shape[1:], 0)
    col_id = lax.broadcasted_iota(jnp.int32, wave.shape[1:], 1)
    ok = (row_id < tables[cols, rows]) & (col_id < tables[cols + 1, rows])
    return jnp.where(ok, wave[t], 0.0)


class Tables:
    def __init__(self, coupling, *sizes):
        self.coupling, self.sizes, self.terms = coupling, sizes, coupling.shape[0]

    def __getitem__(self, at):
        row, sector = at
        if isinstance(row, int) and row >= self.terms:
            return self.sizes[row - self.terms][sector]
        return self.coupling[row, sector]


def first_kernel(plan, coupling_at, left_sizes_at, right_sizes_at, wave, left_ops, right_ops,
                 keep, send_others, send_ours, pieces, packed,
                 coupling, left_sizes, right_sizes, wave_in, left_in, right_in, flipped, a_away,
                 u_pair, total, inverse, sems):
    side, mine, _, my_rep = places(plan)
    tables = Tables(coupling, left_sizes, right_sizes)
    loads = ((wave, wave_in), (right_ops, right_in), (left_ops, left_in), (coupling_at, coupling),
             (left_sizes_at, left_sizes), (right_sizes_at, right_sizes))
    copies = [pltpu.make_async_copy(src, dst, sems.at[i]) for i, (src, dst) in enumerate(loads)]
    for copy in copies:
        copy.start()
    home, right, source = stacks(plan, packed, "home", "right", "source")
    away, = stacks(plan, a_away, "away")
    half_at = pl.multiple_of(side * plan.part, plan.part)
    for i in (3, 4, 5, 0):
        copies[i].wait()
    for t in range(plan.own):
        masked = masked_wave(plan, tables, wave_in, t)
        source.put(t, masked)
        wave_in[t] = masked
    for t in range(plan.own):
        flipped[t] = wave_in[t, :, pl.ds(half_at, plan.part)].T
        for off in range(plan.half):
            at = (lax.rem(mine + off, plan.half) * plan.rep + my_rep) * plan.rows
            value = flipped[t, pl.ds(pl.multiple_of(at, plan.rows), plan.rows), :]
            pieces[off, t * plan.rows:(t + 1) * plan.rows] = value
    copies[1].wait()
    prepare_left(plan, right_in, flipped.at[pl.ds(plan.own, plan.terms)], away, home)
    first_products(plan, away, source, u_pair)
    copies[2].wait()
    prepare_right(plan, left_in, right)
    second_products(plan, tables, inverse, right, u_pair, total)
    hand_out(plan, range(1, plan.half), total, tables, 1, keep, send_others, send_ours)


def home_kernel(rows_are, names, plan, tables, *refs):
    packs, refs = refs[:len(names)], refs[len(names):]
    keep, send_others, send_ours, u_pair, total, inverse = refs
    home, right, source = [found for pack, part in zip(packs, names) for found in stacks(plan, pack, *part)]
    apply_terms(plan, tables, inverse, home, right, source, u_pair, total)
    hand_out(plan, range(1), total, tables, rows_are, keep, send_others, send_ours)


def prepare_kernel(plan, tables, wave, left_ops, right_ops, a_away, packed, turned, flipped):
    home, right = stacks(plan, packed, "home", "right")
    away, = stacks(plan, a_away, "away")
    for t in range(plan.own):
        turned[t] = masked_wave(plan, tables, wave, t).T
    prepare_left(plan, left_ops, flipped, away, home)
    prepare_right(plan, right_ops, right)


def second_kernel(plan, tables, turned, a_away, packed, *rest):
    units, rest = rest[:2 * plan.op], rest[2 * plan.op:]
    (keep, send_others, send_ours, s_pair, full, norm, u_pair, total, inverse) = rest
    _, right = stacks(plan, packed, "home", "right")
    away, = stacks(plan, a_away, "away")
    source, = stacks(plan, s_pair, "source")
    my_op, my_rep = lax.axis_index("op"), lax.axis_index("rep")
    w, rows = plan.width, plan.rows
    sums = sum(unit[plan.piece:] for unit in units)
    entries = plan.sectors * w * w
    sums = jnp.broadcast_to(jnp.sum(sums, axis=1, keepdims=True), sums.shape)
    energy = sums[0:1] / sums[1:2]
    height = 1.0 + jnp.sqrt(sums[2:3] / entries) / TINY
    level = 1.0 / height
    squares = jnp.zeros((TILE, w), F32)
    for whose in range(2):
        r = my_rep if whose == 0 else 1 - my_rep
        for bits in range(plan.op):
            unit = units[whose * plan.op + bits]
            at = pl.multiple_of(((my_op ^ bits) * plan.rep + r) * rows, rows)
            for t in range(plan.own):
                res = unit[t * rows:(t + 1) * rows] - energy * turned[t, pl.ds(at, rows), :]
                squares = squares + jnp.sum(res.reshape(rows // TILE, TILE, w) ** 2, axis=0)
                full[t, pl.ds(at, rows), :] = res
    for t in range(plan.own):
        source.put(t, full[t] * level)
    norm[0:4] = jnp.full((4, w), jnp.sum(squares), F32)
    norm[4:8] = jnp.broadcast_to(height, (4, w))
    apply_terms(plan, tables, inverse, away, right, source, u_pair, total)
    hand_out(plan, range(1, plan.half), total, tables, 0, keep, send_others, send_ours)


def residual_kernel(plan, full, residual, flipped):
    side, mine, _, my_rep = places(plan)
    at = pl.multiple_of((mine * plan.rep + my_rep) * plan.rows, plan.rows)
    for t in range(plan.own):
        flipped[t] = full[t, :, pl.ds(pl.multiple_of(side * plan.part, plan.part), plan.part)].T
        residual[t] = flipped[t, pl.ds(at, plan.rows), :]


def join_kernel(plan, sigma, extra, cross, unit):
    unit[:plan.piece] = sigma[...]
    row = lax.broadcasted_iota(jnp.int32, extra.shape, 0)
    unit[plan.piece:] = extra[...] + jnp.where(row == 0, cross[...], 0.0)


def sums_tile(products, squares, shares):
    rows = [sum(jnp.sum(x, axis=0, keepdims=True) for x in part) for part in (products, squares, shares)]
    return jnp.concatenate(rows + [jnp.zeros((TILE - 3,) + rows[0].shape[1:], F32)])


def gather_along_op(plan, piece, beside):
    if plan.op == 4:
        far = plan.flip_op(piece, 3)
        near = plan.flip_op(piece, 1)
        far, beside = lax.optimization_barrier((far, beside))
        return [piece, near, plan.flip_op(far, 1), far], beside
    got = piece[None]
    for bits in powers(plan.op):
        got = jnp.concatenate([got, plan.flip_op(got, bits)])
    return [got[i] for i in range(plan.op)], beside


def on_device(mesh_shape, wavefunction, left_operators, right_operators, coupling, left_sizes, right_sizes):
    plan = Plan(mesh_shape, wavefunction, left_operators, coupling)
    own, w, rows, terms = plan.own, plan.width, plan.rows, plan.terms
    smem = pl.BlockSpec(memory_space=pltpu.SMEM)
    vmem = pl.BlockSpec(memory_space=pltpu.VMEM)
    hbm = pl.BlockSpec(memory_space=pltpu.HBM)

    def spread(offsets):
        shapes = ((plan.sec, offsets), (plan.sec - 1, offsets), (offsets,))
        return tuple(jax.ShapeDtypeStruct(x + (plan.piece, w), F32) for x in shapes)

    def work(n):
        return [
            pltpu.VMEM((2 * terms, own * n, 2 * w), BF16),
            pltpu.VMEM((plan.sectors, n, w), F32),
            pltpu.SMEM((terms, plan.sectors), jnp.int32),
        ]

    def call(body, n, out_shape, in_specs, scratch, grant=28):
        flops = 3 * 2 * 2 * 2 * terms * own * n * w * w
        return pl.pallas_call(
            functools.partial(body, plan),
            out_shape=out_shape,
            in_specs=in_specs,
            out_specs=(vmem,) * len(out_shape),
            scratch_shapes=scratch,
            compiler_params=pltpu.CompilerParams(vmem_limit_bytes=grant << 20),
            cost_estimate=pl.CostEstimate(flops=flops, bytes_accessed=4 << 20, transcendentals=0),
        )

    blocks = jax.ShapeDtypeStruct((own, w, w), F32)
    def packed(*names):
        return jax.ShapeDtypeStruct(stack_shape(plan, *names), BF16)

    chunks = jax.ShapeDtypeStruct((plan.half, plan.piece, w), F32)
    operators = pltpu.VMEM((terms, w, w), F32)
    turned_operators = pltpu.VMEM((terms, plan.part, w), F32)

    def ring_in_half(parts, at):
        run = parts[at(plan.half - 2)]
        for i in range(plan.half - 3, -1, -1):
            run = plan.next_in_half(run) + parts[at(i)]
        return plan.next_in_half(run)

    def along_half(sums, rows_are, names, home_args, tables):
        keep, send_others, send_ours = sums
        away = keep[1:] + plan.across_cores(send_others)
        away, home_args = lax.optimization_barrier((away, home_args))
        sent = keep[0] + plan.across_cores(send_ours)
        others = ring_in_half(away, lambda i: (slice(None), i))
        kept = call(
            functools.partial(home_kernel, rows_are, names), plan.block, spread(1),
            [smem] + [vmem] * len(names), work(plan.block),
        )(tables, *home_args)
        keep, send_others, send_ours = kept
        others, send_ours = lax.optimization_barrier((others, send_ours))
        others = others + (keep[1:] + plan.across_cores(send_others))[:, 0]
        home = (keep[0] + plan.across_cores(send_ours))[0]
        going, _ = lax.optimization_barrier((sent, keep))
        return others, home, ring_in_half(going, lambda i: i), sent

    def along_sec(others, ours, extra):
        if plan.sec == 2:
            got = plan.next_sec(jnp.concatenate([others[0], extra]))
            return ours + got[:plan.piece], extra + got[plan.piece:], got[:plan.piece]
        run = others[plan.sec - 2]
        for i in range(plan.sec - 3, -1, -1):
            run = plan.next_sec(run) + others[i]
        run = plan.next_sec(run)
        for bits in powers(plan.sec):
            extra = extra + plan.flip_sec(extra, bits)
        return ours + run, extra, run

    *sums, pieces, packs = call(
        first_kernel, plan.away,
        spread(plan.half - 1) + (chunks, packed("home", "right", "source")),
        [hbm] * 6,
        [pltpu.SMEM(x.shape, x.dtype) for x in (coupling, left_sizes, right_sizes)]
        + [pltpu.VMEM(blocks.shape, F32), operators, operators, pltpu.VMEM((own + terms, plan.part, w), F32),
         pltpu.VMEM(packed("away").shape, BF16)] + work(plan.away) + [pltpu.SemaphoreType.DMA((6,))],
    )(*[pltpu.with_memory_space_constraint(x, pltpu.HBM)
        for x in (coupling, left_sizes, right_sizes, wavefunction, left_operators, right_operators)])
    sums, *again = lax.optimization_barrier((sums, coupling, left_sizes, right_sizes))
    tables = jnp.concatenate([again[0], again[1][None], again[2][None]])

    others, home, got, sent = along_half(sums, 1, (("home", "right", "source"),), (packs,), tables)
    extra = sums_tile(
        [home * pieces[0]] + [sent[i] * pieces[1 + i] for i in range(plan.half - 1)], [pieces[0] ** 2],
        [(x * TINY) ** 2 for x in [home, *sent, *others]],
    )
    sigma, extra, crossed = along_sec(others, home + got, extra)
    cross = jnp.sum(crossed * pieces[0], axis=0, keepdims=True)
    if plan.sec == 2:
        cross = 2.0 * cross
    else:
        for bits in powers(plan.sec):
            cross = cross + plan.flip_sec(cross, bits)
    unit, = call(join_kernel, 1, (jax.ShapeDtypeStruct((plan.piece + TILE, w), F32),), [vmem] * 3, [])(
        sigma, extra, cross)

    unit, *again = lax.optimization_barrier((unit, wavefunction, left_operators, right_operators))
    prepared = call(
        prepare_kernel, 1, (packed("away"), packed("home", "right"), blocks), [smem] + [vmem] * 3, [turned_operators],
    )(tables, *again)
    units, (a_away, packs, turned) = gather_along_op(plan, unit, prepared)
    units = units + [plan.across_cores(x) for x in units]

    *sums, s_pair, full, norm = call(
        second_kernel, plan.away,
        spread(plan.half - 1) + (packed("source"), blocks, jax.ShapeDtypeStruct((TILE, w), F32)),
        [smem] + [vmem] * (3 + len(units)),
        work(plan.away),
    )(tables, turned, a_away, packs, *units)

    others, home, got, _ = along_half(sums, 0, (("home", "right"), ("source",)), (packs, s_pair), tables)
    residual, = call(residual_kernel, 1, (jax.ShapeDtypeStruct((own, rows, w), F32),), [vmem],
                     [pltpu.VMEM((own, plan.part, w), F32)])(full)
    sigma, total, _ = along_sec(others, home + got, norm)
    sigma, residual = lax.optimization_barrier((sigma, residual))
    entries = plan.sectors * w * w
    factor = norm[4:5] / jnp.sqrt(total[0:1] / entries + 1e-06)
    sigma_next = (sigma * factor).reshape(own, rows, w)
    return (sigma_next, residual)


def solution(mesh):
    in_specs = (
        P(("grp", "sec"), None, None),
        P(("op", "rep"), None, None),
        P(("op", "rep"), None, None),
        P(("op", "rep"), None),
        P("grp"),
        P("grp"),
    )
    out_specs = (P(("grp", "sec"), ("op", "rep"), None), P(("grp", "sec"), ("op", "rep"), None))
    return jax.shard_map(
        functools.partial(on_device, dict(mesh.shape)),
        mesh=mesh, in_specs=in_specs, out_specs=out_specs, check_vma=False,
    )
```
